512 devices in a mesh: sample: 16 (over y, z_hi), head: 32 (over z_lo, x, core).
Axes of the slice: x: 4, y: 4, z: 16 (z_hi: 4, z_lo: 4; z = z_hi * 4 + z_lo), core: 2. Of those that a mesh axis runs over, the one named last changes fastest.
Arguments:
- queries: bfloat16 [65536, 4096], P(('sample', 'head')), may hold values from -6 to 6
- keys: bfloat16 [65536, 1024], P(('sample', 'head')), may hold values from -6 to 6
- values: bfloat16 [65536, 1024], P(('sample', 'head')), may hold values from -6 to 6
- cotangent: bfloat16 [65536, 4096], P(('sample', 'head')), may hold values from -6 to 6
- prompt_keys: bfloat16 [8, 512, 128], P(None, 'sample'), may hold values from -6 to 6
- prompt_values: bfloat16 [8, 512, 128], P(None, 'sample'), may hold values from -6 to 6
- response_ids: int32 [16, 4096], P('sample'), may hold values from 0 to 31, never falling along the last dimension, each value on 1 to 256 neighbouring positions
- block_pattern: int32 [16, 32, 32], P('sample'), may hold values 0 or 1
Outputs:
- grad_queries: bfloat16 [65536, 4096], P(('sample', 'head'))
- grad_keys: bfloat16 [65536, 1024], P(('sample', 'head'))
- grad_values: bfloat16 [65536, 1024], P(('sample', 'head'))
The draws below stay inside these ranges and needn't reach their ends.
Inputs may be any that keep to these rules, and one draw needn't show every extreme that they name: `response_ids`: along a group's 4096 positions the response number never falls; each response holds 1 to 256 positions and one holds exactly 256.
All inputs are finite; a program needn't handle non-finite values. No bound on the sum of `block_pattern` on one device may be relied on, other than what follows from the above.
Results may differ from the reference program's by a relative error of at most 0.022.
Values may be sent and summed in bfloat16 or wider, within the bound.
A program may use at most 64 MiB of HBM per device.

```python
import math
import jax
import jax.numpy as jnp
import numpy as np
from jax import lax

HEADS = 32
KVH = 8
HD = 128
MOST = 256
BLOCK = 128
QB = 512
GROUP_TOK = 4096
TOKENS = 65536
PROMPT = 512
NBLK = 32
N_SAMPLE = 16


def draw_queries(key, part):
    key = jax.random.fold_in(key, 5)
    drawn = jnp.clip(jax.random.normal(key, (TOKENS, HEADS * HD), jnp.float32), -6.0, 6.0)
    return drawn.astype(jnp.bfloat16)


def draw_prompt_keys(key, part):
    key = jax.random.fold_in(key, 9)
    drawn = jnp.clip(jax.random.normal(key, (KVH, PROMPT, HD), jnp.float32), -6.0, 6.0)
    return drawn.astype(jnp.bfloat16)


def place_ends(values, stream_key, least, top_value):
    longest = values.shape.index(max(values.shape))
    spots = []
    for shift in (0, 1):
        where = [jax.random.randint(jax.random.fold_in(stream_key, axis), (), 0, length) for axis, length in enumerate(values.shape)]
        where[longest] = (where[longest] + shift) % values.shape[longest]
        spots.append(tuple(where))
    return values.at[spots[0]].set(least).at[spots[1]].set(top_value)


def block_scale(stream_key, dims, cuts, least, high):
    loudness = 1.0
    for dim, blocks in cuts:
        steps = jax.random.uniform(jax.random.fold_in(jax.random.fold_in(stream_key, 6), dim), (blocks,), jnp.float32, least / len(cuts), high / len(cuts))
        loudness = loudness * jnp.repeat(jnp.exp(steps), dims[dim] // blocks).reshape((-1,) + (1,) * (len(dims) - 1 - dim))
    return loudness


def length_profile(number_of, total, bound, skew):
    weights = [(1 << 20) // math.isqrt(rank ** skew) + 1 for rank in range(2, number_of + 1)]
    rest, given = total - bound - (number_of - 1), [1] * (number_of - 1)
    while rest > 0:
        free = [i for i in range(number_of - 1) if given[i] < bound]
        pool, remaining = sum([weights[i] for i in free]), rest
        for i in free:
            addition = min(bound - given[i], max(1, remaining * weights[i] // pool), rest)
            given[i] = given[i] + addition
            rest = rest - addition
    return np.array([bound] + given)


def ragged(own_key, amount, total, limit, slope):
    if amount == 2:
        one = jax.random.randint(own_key, (), max(1, total - limit), min(limit, total - 1) + 1)
        return jnp.stack([one, total - one])
    tallies = jnp.asarray(length_profile(amount, total, limit, slope), jnp.int32)
    twos = (amount - 1) // 2
    giver, taker = tallies[1:1 + 2 * twos:2], tallies[2:2 + 2 * twos:2]
    room = jnp.minimum(giver - 1, limit - taker)
    shifted = jax.random.randint(jax.random.fold_in(own_key, 1), (twos,), 0, 1 << 20) % (room + 1)
    tallies = tallies.at[1:1 + 2 * twos:2].set(giver - shifted).at[2:2 + 2 * twos:2].set(taker + shifted)
    return tallies[jax.random.permutation(jax.random.fold_in(own_key, 2), amount)]


def gaussian(key, dims, scale, bound, pieces=(), held_as=jnp.bfloat16):
    entries = scale * jax.random.normal(key, dims, jnp.float32)
    if pieces:
        entries = entries * block_scale(key, dims, pieces, -0.22, 0.18)
    return jnp.clip(entries, -bound, bound).astype(held_as)


def setup_inputs(seed: int = 0) -> dict:
    key_list = jax.random.split(jax.random.key(seed), 9)
    return {
        "queries": draw_queries(jax.random.fold_in(key_list[8], 71), 0),
        "keys": gaussian(key_list[1], (TOKENS, KVH * HD), 1.0, 6.0, ((0, 512),)),
        "values": gaussian(key_list[2], (TOKENS, KVH * HD), 1.0, 6.0, ((0, 512),)),
        "cotangent": gaussian(key_list[3], (TOKENS, HEADS * HD), 1.0, 6.0, ((0, 512),)),
        "prompt_keys": draw_prompt_keys(jax.random.fold_in(key_list[8], 71), 0),
        "prompt_values": gaussian(key_list[5], (KVH, PROMPT, HD), 1.0, 6.0, ((1, 16),)),
        "response_ids": jax.vmap(lambda own: jnp.searchsorted(jnp.cumsum(ragged(own, NBLK, GROUP_TOK, MOST, 2)), jnp.arange(GROUP_TOK), side="right"))(jax.random.split(key_list[6], N_SAMPLE)).reshape((N_SAMPLE, GROUP_TOK)).astype(jnp.int32),
        "block_pattern": place_ends((jax.random.randint(key_list[7], (N_SAMPLE, NBLK, NBLK), 0, 4) < 3).astype(jnp.int32), jax.random.fold_in(key_list[7], 1), 0, 1),
    }


def padded_tables(id_row, pattern, back):
    nblocks = pattern.shape[0]
    blocks = jnp.maximum(pattern, jnp.eye(nblocks, dtype=jnp.int32))
    blk_pad = jnp.concatenate([jnp.zeros((nblocks, back // BLOCK), jnp.int32), blocks], 1)
    id_pad = jnp.concatenate([jnp.full((back,), -1, jnp.int32), id_row.astype(jnp.int32)])
    return id_pad, blk_pad


def window_mask(id_pad, blk_pad, back, start, rows_count, keys_count):
    start = start.astype(jnp.int32)
    row_ids = lax.dynamic_slice_in_dim(id_pad, start + back, rows_count)
    key_ids = lax.dynamic_slice_in_dim(id_pad, start, keys_count)
    rows = start + jnp.arange(rows_count, dtype=jnp.int32)
    places = start - back + jnp.arange(keys_count, dtype=jnp.int32)
    first = start // BLOCK
    sub = lax.dynamic_slice(blk_pad, (first, first), (rows_count // BLOCK, keys_count // BLOCK))
    spread = jnp.repeat(jnp.repeat(sub, BLOCK, 0), BLOCK, 1)
    return (row_ids[:, None] == key_ids[None, :]) & (places[None, :] <= rows[:, None]) & (spread > 0)


def tile_grads(query, upstream, first_keys, first_values, near_keys, near_values, allowed):
    scale = query.shape[-1] ** -0.5
    width = first_keys.shape[0]
    all_keys = jnp.concatenate([first_keys, near_keys], 0).astype(jnp.float32)
    all_values = jnp.concatenate([first_values, near_values], 0).astype(jnp.float32)
    query_f = query.astype(jnp.float32)
    upstream_f = upstream.astype(jnp.float32)
    scores = jnp.einsum("rgd,kd->grk", query_f, all_keys) * scale
    visible = jnp.concatenate([jnp.ones((allowed.shape[0], width), jnp.bool_), allowed], 1)[None]
    scores = jnp.where(visible, scores, -1e30)
    peak = jnp.max(scores, -1, keepdims=True)
    expo = jnp.where(visible, jnp.exp(scores - peak), 0.0)
    weights = expo / jnp.sum(expo, -1, keepdims=True)
    dweights = jnp.einsum("rgd,kd->grk", upstream_f, all_values)
    center = jnp.sum(weights * dweights, -1, keepdims=True)
    dscores = (weights * (dweights - center) * scale).astype(jnp.bfloat16).astype(jnp.float32)
    rounded = weights.astype(jnp.bfloat16).astype(jnp.float32)
    grad_query = jnp.einsum("grk,kd->rgd", dscores, all_keys)
    grad_keys = jnp.einsum("grk,rgd->kd", dscores[:, :, width:], query_f)
    grad_values = jnp.einsum("grk,rgd->kd", rounded[:, :, width:], upstream_f)
    return grad_query, grad_keys, grad_values


def reference(queries, keys, values, cotangent, prompt_keys, prompt_values, response_ids, block_pattern):
    group = HEADS // KVH
    all_q = queries.reshape(N_SAMPLE, GROUP_TOK, KVH, group, HD)
    all_u = cotangent.reshape(N_SAMPLE, GROUP_TOK, KVH, group, HD)
    all_k = keys.reshape(N_SAMPLE, GROUP_TOK, KVH, HD)
    all_v = values.reshape(N_SAMPLE, GROUP_TOK, KVH, HD)

    def one_group(items):
        grp_q, grp_u, grp_k, grp_v, grp_ids, grp_pat = items
        id_pad, blk_pad = padded_tables(grp_ids, grp_pat, MOST)
        key_pad = jnp.concatenate([jnp.zeros((MOST, KVH, HD), jnp.bfloat16), grp_k], 0)
        value_pad = jnp.concatenate([jnp.zeros((MOST, KVH, HD), jnp.bfloat16), grp_v], 0)

        def step(carry, index):
            acc_k, acc_v = carry
            start = (index * QB).astype(jnp.int32)
            block_q = lax.dynamic_slice_in_dim(grp_q, start, QB)
            block_u = lax.dynamic_slice_in_dim(grp_u, start, QB)
            near_k = lax.dynamic_slice_in_dim(key_pad, start, QB + MOST)
            near_v = lax.dynamic_slice_in_dim(value_pad, start, QB + MOST)
            allowed = window_mask(id_pad, blk_pad, MOST, start, QB, QB + MOST)

            def per_head(parts):
                return tile_grads(parts[0], parts[1], parts[2], parts[3], parts[4], parts[5], allowed)

            grad_q, grad_k, grad_v = lax.map(per_head, (block_q.transpose(1, 0, 2, 3), block_u.transpose(1, 0, 2, 3), prompt_keys, prompt_values, near_k.transpose(1, 0, 2), near_v.transpose(1, 0, 2)))
            acc_k = lax.dynamic_update_slice_in_dim(acc_k, lax.dynamic_slice_in_dim(acc_k, start, QB + MOST) + grad_k.transpose(1, 0, 2), start, 0)
            acc_v = lax.dynamic_update_slice_in_dim(acc_v, lax.dynamic_slice_in_dim(acc_v, start, QB + MOST) + grad_v.transpose(1, 0, 2), start, 0)
            return (acc_k, acc_v), grad_q.transpose(1, 0, 2, 3).astype(jnp.bfloat16)

        empty = jnp.zeros((GROUP_TOK + MOST, KVH, HD), jnp.float32)
        (acc_k, acc_v), grad_blocks = lax.scan(step, (empty, empty), jnp.arange(GROUP_TOK // QB, dtype=jnp.int32))
        grad_q = grad_blocks.reshape(GROUP_TOK, HEADS * HD)
        grad_k = acc_k[MOST:].reshape(GROUP_TOK, KVH * HD).astype(jnp.bfloat16)
        grad_v = acc_v[MOST:].reshape(GROUP_TOK, KVH * HD).astype(jnp.bfloat16)
        return grad_q, grad_k, grad_v

    grad_q, grad_k, grad_v = lax.map(one_group, (all_q, all_u, all_k, all_v, response_ids, block_pattern))
    return grad_q.reshape(TOKENS, HEADS * HD), grad_k.reshape(TOKENS, KVH * HD), grad_v.reshape(TOKENS, KVH * HD)
```

```python
import math

import jax
import jax.numpy as jnp
from jax import lax
from jax.experimental import pallas as pl
from jax.experimental.pallas import tpu as pltpu
from jax.sharding import PartitionSpec as P

KVH = 8
HD = 128
BLK = 128
SCALE = HD**-0.5
SCALE2 = SCALE * math.log2(math.e)
HIDE = -1e30
MESH = pl.DeviceIdType.MESH
BF = jnp.bfloat16
F32 = jnp.float32

NT = (((1,), (1,)), ((), ()))
NN = (((1,), (0,)), ((), ()))


def dot(a, b, dims):
    return lax.dot_general(a, b, dims, preferred_element_type=F32)


def tile_grads(q, u, pk, pv, kw, vw, bias, pk_t, kw_t):
    bias = jnp.concatenate([bias] * 4, 1)
    sp = dot(pk, q, NT) * SCALE2
    sw = dot(kw, q, NT) * SCALE2 + bias
    peak = jnp.maximum(jnp.max(sp, 0, keepdims=True), jnp.max(sw, 0, keepdims=True))
    ep = jnp.exp2(sp - peak)
    ew = jnp.exp2(sw - peak)
    inv = 1.0 / (jnp.sum(ep, 0, keepdims=True) + jnp.sum(ew, 0, keepdims=True))
    dp = dot(pv, u, NT)
    dw = dot(vw, u, NT)
    center = (jnp.sum(ep * dp, 0, keepdims=True) + jnp.sum(ew * dw, 0, keepdims=True)) * inv
    inv_s = inv * SCALE
    dsp = ((ep * inv_s) * (dp - center)).astype(BF)
    dsw = ((ew * inv_s) * (dw - center)).astype(BF)
    w = (ew * inv).astype(BF)
    gq = (dot(pk_t, dsp, NN) + dot(kw_t, dsw, NN)).T
    return gq, dot(dsw, q, NN), dot(w, u, NN)


def kernel(
    q_hbm, u_hbm, k_hbm, v_hbm, pk_hbm, pv_hbm, ids_hbm, pat_hbm,
    gq_hbm, gk_hbm, gv_hbm,
    ids, pat, bias, qb, ub, kw, vw, pkv, gs, gown, gnext, gqb, fin,
    sem_in, sem_small, sem_own,
    snd_a, rcv_a, snd_b, rcv_b, snd_c1, rcv_c1, snd_c2, rcv_c2,
    snd_sib, rcv_sib, snd_halo, rcv_halo, snd_gq, rcv_gq, sem_gq,
    snd_gsib, rcv_gsib, snd_gprev, rcv_gnext, sem_out,
):
    s = lax.axis_index("sample")
    hd = lax.axis_index("head")
    y, zh = s // 4, s % 4
    c, k = hd // 2, hd % 2
    zl = hd // 8
    first, last = c == 0, c == 15
    sib = (s, c * 2 + (1 - k))
    nxt = [(s, jnp.minimum(c + 1, 15) * 2 + i) for i in range(2)]
    prv = [(s, jnp.maximum(c - 1, 0) * 2 + i) for i in range(2)]
    zh_at = [lax.rem(zh + d, 4) for d in range(4)]
    zh_peer = [(y * 4 + zh_at[d], hd) for d in range(4)]
    zl_peer = [(s, lax.rem(hd + 8 * d, 32)) for d in range(4)]
    up, down, over = lax.rem(y + 1, 4), lax.rem(y + 3, 4), lax.rem(y + 2, 4)
    y_up, y_down = (up * 4 + zh, hd), (down * 4 + zh, hd)
    rows = pl.ds(pl.multiple_of(k * BLK, BLK), BLK)
    other = pl.ds(pl.multiple_of((1 - k) * BLK, BLK), BLK)
    own_rows = pl.ds(pl.multiple_of(256 + k * BLK, BLK), BLK)
    sib_rows = pl.ds(pl.multiple_of(256 + (1 - k) * BLK, BLK), BLK)

    def cols(core, h, width):
        return pl.ds(pl.multiple_of((core * 4 + h) * width, BLK), width)

    def send(src, dst, snd, rcv, where):
        return pltpu.make_async_remote_copy(
            src_ref=src, dst_ref=dst, send_sem=snd, recv_sem=rcv, device_id=where, device_id_type=MESH
        )

    barrier = pltpu.get_barrier_semaphore()

    def greet(where):
        pl.semaphore_signal(barrier, inc=1, device_id=where, device_id_type=MESH)

    for where in [sib] + zh_peer[1:] + zl_peer[1:] + [y_up, y_down]:
        greet(where)

    @pl.when(jnp.logical_not(last))
    def _():
        greet(nxt[0])
        greet(nxt[1])

    @pl.when(jnp.logical_not(first))
    def _():
        greet(prv[0])
        greet(prv[1])

    own_prompt = [
        pltpu.make_async_copy(src.at[pl.ds(k * 4, 4)], pkv.at[:, i, y, zh], sem_small.at[i])
        for i, src in enumerate((pk_hbm, pv_hbm))
    ]
    for copy in own_prompt:
        copy.start()
    small = [
        pltpu.make_async_copy(ids_hbm, ids, sem_small.at[2]),
        pltpu.make_async_copy(pat_hbm, pat, sem_small.at[3]),
    ]
    for copy in small:
        copy.start()

    def own_parts(h):
        return [
            pltpu.make_async_copy(q_hbm.at[:, cols(k, h, 512)], qb.at[h, rows], sem_in.at[h, 0]),
            pltpu.make_async_copy(u_hbm.at[:, cols(k, h, 512)], ub.at[h, rows], sem_in.at[h, 1]),
            pltpu.make_async_copy(k_hbm.at[:, cols(k, h, 128)], kw.at[h, own_rows], sem_in.at[h, 2]),
            pltpu.make_async_copy(v_hbm.at[:, cols(k, h, 128)], vw.at[h, own_rows], sem_in.at[h, 3]),
        ]

    for h in range(4):
        for copy in own_parts(h):
            copy.start()

    others = 9 + 2 * jnp.where(first, 0, 1) + 2 * jnp.where(last, 0, 1)
    pl.semaphore_wait(barrier, others)

    def part_a(d, i):
        src = (pk_hbm, pv_hbm)[i].at[k * 4 + zl]
        return send(src, pkv.at[zl, i, y, zh], snd_a.at[d, i], rcv_a.at[d, i], zh_peer[d])

    for d in (1, 3, 2):
        for i in range(2):
            part_a(d, i).start()

    def to_sib(h):
        far = 1 - k
        return [
            send(q_hbm.at[:, cols(far, h, 512)], qb.at[h, rows], snd_sib.at[h, 0], rcv_sib.at[h, 0], sib),
            send(u_hbm.at[:, cols(far, h, 512)], ub.at[h, rows], snd_sib.at[h, 1], rcv_sib.at[h, 1], sib),
            send(k_hbm.at[:, cols(far, h, 128)], kw.at[h, own_rows], snd_sib.at[h, 2], rcv_sib.at[h, 2], sib),
            send(v_hbm.at[:, cols(far, h, 128)], vw.at[h, own_rows], snd_sib.at[h, 3], rcv_sib.at[h, 3], sib),
        ]

    def halo(h, core, i):
        src, dst = ((k_hbm, kw), (v_hbm, vw))[i]
        return send(
            src.at[:, cols(core, h, 128)], dst.at[h, rows], snd_halo.at[h, core, i], rcv_halo.at[h, k, i], nxt[core]
        )

    for h in range(4):
        for copy in to_sib(h):
            copy.start()

        @pl.when(jnp.logical_not(last))
        def _(h=h):
            for core in range(2):
                for i in range(2):
                    halo(h, core, i).start()

    @pl.when(first)
    def _():
        kw[:, 0:256] = jnp.zeros((4, 256, HD), BF)
        vw[:, 0:256] = jnp.zeros((4, 256, HD), BF)

    @pl.when(last)
    def _():
        gnext[...] = jnp.zeros((8, 2, BLK, HD), BF)

    for copy in small:
        copy.wait()
    base = jnp.maximum(c - 1, 0) * 256
    id_rows = [
        ids[:, pl.ds(pl.multiple_of(base + b * BLK, BLK), BLK)].astype(F32) for b in range(2)
    ] + [ids[:, pl.ds(pl.multiple_of(c * 256 + b * BLK, BLK), BLK)].astype(F32) for b in range(2)]
    wide = [jnp.broadcast_to(r, (BLK, BLK)) for r in id_rows]
    tall = [w.T for w in wide]
    key_at = lax.broadcasted_iota(jnp.int32, (BLK, BLK), 0)
    row_at = lax.broadcasted_iota(jnp.int32, (BLK, BLK), 1)
    inside = jnp.where(first, 0, 1)
    for rb in range(2):
        at = 2 * c + rb
        for t in range(3):
            b = rb + t
            seen = tall[b] == wide[2 + rb]
            if t == 2:
                seen = seen & (key_at <= row_at)
            else:
                flag = pat[0, at, jnp.maximum(at - 2 + t, 0)]
                if b < 2:
                    flag = flag * inside
                seen = seen & (jnp.full((BLK, BLK), flag, jnp.int32) > 0)
            bias[rb, t * BLK : (t + 1) * BLK] = jnp.where(seen, 0.0, HIDE)

    def part_b(d, e):
        part = pkv.at[zl, :, y, zh_at[e]]
        return send(part, part, snd_b.at[d, e], rcv_b.at[zl, e], zl_peer[d])

    for copy in own_prompt:
        copy.wait()
    for e in (3, 1, 2):
        for i in range(2):
            part_a(4 - e, i).wait_recv()
        for d in (1, 3, 2):
            part_b(d, e).start()

    def part_c1(h, to):
        part = pkv.at[h, :, y]
        return send(part, part, snd_c1.at[h, to], rcv_c1.at[h, to], (y_up, y_down)[to])

    def c1_of(h, to, at):
        part = pkv.at[h, :, at]
        return send(part, part, snd_c1.at[h, to], rcv_c1.at[h, to], (y_up, y_down)[to])

    for h in range(4):

        @pl.when(zl != h)
        def _(h=h):
            for e in (3, 1, 2):
                part = pkv.at[h, :, y, zh_at[e]]
                send(part, part, snd_b.at[1, e], rcv_b.at[h, e], zl_peer[1]).wait_recv()

        for to in range(2):
            part_c1(h, to).start()

    def part_c2(h, to, at):
        part = pkv.at[h, to, at]
        return send(part, part, snd_c2.at[h, to], rcv_c2.at[h, to], (y_up, y_down)[to])

    def relay(h):
        c1_of(h, 0, down).wait_recv()
        part_c2(h, 0, down).start()
        c1_of(h, 1, up).wait_recv()
        part_c2(h, 1, up).start()

    def to_prev(h, core):
        part = gs.at[h, :, core * BLK : (core + 1) * BLK]
        return send(part, gnext.at[k * 4 + h], snd_gprev.at[h, core], rcv_gnext.at[k * 4 + h], prv[core])

    def grads_to_sib(h):
        return send(gs.at[h, :, sib_rows], gown.at[k * 4 + h], snd_gsib.at[h], rcv_gsib.at[h], sib)

    def gq_own(h):
        return pltpu.make_async_copy(gqb.at[h, rows], gq_hbm.at[:, cols(k, h, 512)], sem_gq.at[h])

    def gq_to_sib(h):
        return send(gqb.at[h, other], gq_hbm.at[:, cols(k, h, 512)], snd_gq.at[h], rcv_gq.at[h], sib)

    relay(0)

    @pl.loop(0, 4)
    def _(h):
        @pl.when(h < 3)
        def _():
            relay(h + 1)

        for copy in own_parts(h):
            copy.wait()
        for copy in to_sib(h):
            copy.wait_recv()
        for to in range(2):
            part_c2(h, to, over).wait_recv()

        @pl.when(jnp.logical_not(first))
        def _():
            for core in range(2):
                for i in range(2):
                    dst = (kw, vw)[i].at[h, core * BLK : (core + 1) * BLK]
                    send(dst, dst, snd_halo.at[h, core, i], rcv_halo.at[h, core, i], prv[0]).wait_recv()

        pk = pkv[h, 0].reshape(512, HD)
        pv = pkv[h, 1].reshape(512, HD)
        pk_t = pk.T
        kw_t = kw[h].T
        parts = []
        for rb in range(2):
            qr = qb[h, rb * BLK : (rb + 1) * BLK]
            ur = ub[h, rb * BLK : (rb + 1) * BLK]
            q = jnp.concatenate([qr[:, g * HD : (g + 1) * HD] for g in range(4)], 0)
            u = jnp.concatenate([ur[:, g * HD : (g + 1) * HD] for g in range(4)], 0)
            near = slice(rb * BLK, rb * BLK + 384)
            gq, gk, gv = tile_grads(q, u, pk, pv, kw[h, near], vw[h, near], bias[rb], pk_t, kw_t[:, near])
            for g in range(4):
                gqb[h, rb * BLK : (rb + 1) * BLK, g * HD : (g + 1) * HD] = gq[g * BLK : (g + 1) * BLK].astype(BF)
            parts.append((gk, gv))
        for i in range(2):
            a, b = parts[0][i], parts[1][i]
            gs[h, i, 0:128] = a[0:128].astype(BF)
            gs[h, i, 128:384] = (a[128:384] + b[0:256]).astype(BF)
            gs[h, i, 384:512] = b[256:384].astype(BF)

        @pl.when(jnp.logical_not(first))
        def _():
            for core in range(2):
                to_prev(h, core).start()

        grads_to_sib(h).start()
        gq_to_sib(h).start()
        gq_own(h).start()
        gown[k * 4 + h] = gs[h, :, own_rows]

    def outs(hh):
        return [
            pltpu.make_async_copy(fin.at[hh, i], out.at[:, hh * HD : (hh + 1) * HD], sem_out.at[hh, i])
            for i, out in enumerate((gk_hbm, gv_hbm))
        ]

    for h in range(4):
        send(gs.at[h, :, sib_rows], gown.at[(1 - k) * 4 + h], snd_gsib.at[h], rcv_gsib.at[h], sib).wait_recv()
        for core in range(2):

            @pl.when(jnp.logical_not(last))
            def _(core=core, h=h):
                part = gnext.at[core * 4 + h]
                send(part, part, snd_gprev.at[h, core], rcv_gnext.at[core * 4 + h], nxt[0]).wait_recv()

            hh = core * 4 + h
            fin[hh] = (gown[hh].astype(F32) + gnext[hh].astype(F32)).astype(BF)
            for copy in outs(hh):
                copy.start()

    for h in range(4):
        gq_own(h).wait()
        copy = gq_to_sib(h)
        copy.wait_send()
        send(gqb.at[h, rows], gq_hbm.at[:, cols(1 - k, h, 512)], snd_gq.at[h], rcv_gq.at[h], sib).wait_recv()
        grads_to_sib(h).wait_send()
        for copy in to_sib(h):
            copy.wait_send()
        for to in range(2):
            part_c1(h, to).wait_send()
        part_c2(h, 0, down).wait_send()
        part_c2(h, 1, up).wait_send()

    for d in (1, 2, 3):
        for i in range(2):
            part_a(d, i).wait_send()
        for e in (1, 2, 3):
            part_b(d, e).wait_send()

    @pl.when(jnp.logical_not(last))
    def _():
        for h in range(4):
            for core in range(2):
                for i in range(2):
                    halo(h, core, i).wait_send()

    @pl.when(jnp.logical_not(first))
    def _():
        for h in range(4):
            for core in range(2):
                to_prev(h, core).wait_send()

    for hh in range(KVH):
        for copy in outs(hh):
            copy.wait()


def shards(queries, keys, values, cotangent, prompt_keys, prompt_values, response_ids, block_pattern):
    anywhere = pl.BlockSpec(memory_space=pl.ANY)
    dma = pltpu.SemaphoreType.DMA
    return pl.pallas_call(
        kernel,
        out_shape=[
            jax.ShapeDtypeStruct(queries.shape, BF),
            jax.ShapeDtypeStruct(keys.shape, BF),
            jax.ShapeDtypeStruct(values.shape, BF),
        ],
        in_specs=[anywhere] * 8,
        out_specs=[anywhere] * 3,
        scratch_shapes=[
            pltpu.VMEM((1, 4096), jnp.int32),
            pltpu.SMEM((1, 32, 32), jnp.int32),
            pltpu.VMEM((2, 384, BLK), F32),
            pltpu.VMEM((4, 256, 512), BF),
            pltpu.VMEM((4, 256, 512), BF),
            pltpu.VMEM((4, 512, HD), BF),
            pltpu.VMEM((4, 512, HD), BF),
            pltpu.VMEM((4, 2, 4, 4, 32, HD), BF),
            pltpu.VMEM((4, 2, 512, HD), BF),
            pltpu.VMEM((8, 2, BLK, HD), BF),
            pltpu.VMEM((8, 2, BLK, HD), BF),
            pltpu.VMEM((4, 256, 512), BF),
            pltpu.VMEM((8, 2, BLK, HD), BF),
            dma((4, 4)), dma((4,)), dma((1,)),
            dma((4, 2)), dma((4, 2)), dma((4, 4)), dma((4, 4)), dma((4, 2)), dma((4, 2)), dma((4, 2)), dma((4, 2)),
            dma((4, 4)), dma((4, 4)), dma((4, 2, 2)), dma((4, 2, 2)), dma((4,)), dma((4,)), dma((4,)),
            dma((4,)), dma((4,)), dma((4, 2)), dma((8,)), dma((8, 2)),
        ],
        compiler_params=pltpu.CompilerParams(
            collective_id=0, has_side_effects=True, vmem_limit_bytes=48 << 20
        ),
        cost_estimate=pl.CostEstimate(flops=4 << 30, bytes_accessed=8 << 20, transcendentals=4 << 20),
        name="tree_attention_backward",
    )(queries, cotangent, keys, values, prompt_keys, prompt_values, response_ids, block_pattern)


def solution(mesh):
    tokens = P(("sample", "head"), None)
    prompt = P(None, "sample", None)
    return jax.shard_map(
        shards,
        mesh=mesh,
        in_specs=(tokens, tokens, tokens, tokens, prompt, prompt, P("sample", None), P("sample", None, None)),
        out_specs=(tokens, tokens, tokens),
        check_vma=False,
    )
```

```python
import math

import jax
import jax.numpy as jnp
from jax import lax
from jax.experimental import pallas as pl
from jax.experimental.pallas import tpu as pltpu
from jax.sharding import PartitionSpec as P

KVH = 8
HD = 128
BLK = 128
SCALE = HD**-0.5
SCALE2 = SCALE * math.log2(math.e)
HIDE = -1e30
MESH = pl.DeviceIdType.MESH
BF = jnp.bfloat16
F32 = jnp.float32

NT = (((1,), (1,)), ((), ()))
NN = (((1,), (0,)), ((), ()))


def dot(a, b, dims):
    return lax.dot_general(a, b, dims, preferred_element_type=F32)


def tile_grads(q, u, pk, pv, kw, vw, bias, pk_t, kw_t):
    bias = jnp.concatenate([bias] * 4, 1)
    sp = dot(pk, q, NT) * SCALE2
    sw = dot(kw, q, NT) * SCALE2 + bias
    peak = jnp.maximum(jnp.max(sp, 0, keepdims=True), jnp.max(sw, 0, keepdims=True))
    ep = jnp.exp2(sp - peak)
    ew = jnp.exp2(sw - peak)
    inv = 1.0 / (jnp.sum(ep, 0, keepdims=True) + jnp.sum(ew, 0, keepdims=True))
    dp = dot(pv, u, NT)
    dw = dot(vw, u, NT)
    center = (jnp.sum(ep * dp, 0, keepdims=True) + jnp.sum(ew * dw, 0, keepdims=True)) * inv
    inv_s = inv * SCALE
    dsp = ((ep * inv_s) * (dp - center)).astype(BF)
    dsw = ((ew * inv_s) * (dw - center)).astype(BF)
    w = (ew * inv).astype(BF)
    gq = (dot(pk_t, dsp, NN) + dot(kw_t, dsw, NN)).T
    return gq, dot(dsw, q, NN), dot(w, u, NN)


def kernel(
    q_hbm, u_hbm, k_hbm, v_hbm, pk_hbm, pv_hbm, ids_hbm, pat_hbm,
    gq_hbm, gk_hbm, gv_hbm,
    ids, pat, bias, qb, ub, kw, vw, pkv, gs, gown, gnext, gqb, fin, acc,
    sem_in, sem_small, sem_own,
    snd_own, rcv_own, snd_z, rcv_z, snd_c, rcv_c,
    snd_sib, rcv_sib, snd_halo, rcv_halo, snd_gq, rcv_gq, sem_gq,
    snd_gsib, rcv_gsib, snd_gprev, rcv_gnext, sem_out,
):
    s = lax.axis_index("sample")
    hd = lax.axis_index("head")
    y, zh = s // 4, s % 4
    c, k = hd // 2, hd % 2
    zl, x = hd // 8, c % 4
    first, last = c == 0, c == 15
    sib = (s, c * 2 + (1 - k))
    nxt = [(s, jnp.minimum(c + 1, 15) * 2 + i) for i in range(2)]
    prv = [(s, jnp.maximum(c - 1, 0) * 2 + i) for i in range(2)]
    column = lax.rem(hd, 8)

    def along_z(d, to_zl):
        return (y * 4 + lax.rem(zh + d, 4), to_zl * 8 + column)

    y_peer = [(lax.rem(y + d, 4) * 4 + zh, hd) for d in range(4)]
    rows = pl.ds(pl.multiple_of(k * BLK, BLK), BLK)
    other = pl.ds(pl.multiple_of((1 - k) * BLK, BLK), BLK)
    own_rows = pl.ds(pl.multiple_of(256 + k * BLK, BLK), BLK)
    sib_rows = pl.ds(pl.multiple_of(256 + (1 - k) * BLK, BLK), BLK)

    def cols(core, h, width):
        return pl.ds(pl.multiple_of((core * 4 + h) * width, BLK), width)

    def send(src, dst, snd, rcv, where):
        return pltpu.make_async_remote_copy(
            src_ref=src, dst_ref=dst, send_sem=snd, recv_sem=rcv, device_id=where, device_id_type=MESH
        )

    barrier = pltpu.get_barrier_semaphore()

    def greet(where):
        pl.semaphore_signal(barrier, inc=1, device_id=where, device_id_type=MESH)

    upwards = [(2, 2, 1), (2, 2, 0), (3, 1, 3), (3, 1, 2), (3, 1, 1), (3, 1, 0)]
    downwards = [(2, 2, 2), (2, 2, 3), (1, 3, 0), (1, 3, 1), (1, 3, 2), (1, 3, 3)]
    source = {1: along_z(1, 0), 2: along_z(2, jnp.where(zl < 2, 3, 0)), 3: along_z(3, 3)}
    for where in [sib] + y_peer[1:] + list(source.values()):
        greet(where)

    @pl.when(jnp.logical_not(last))
    def _():
        greet(nxt[0])
        greet(nxt[1])

    @pl.when(jnp.logical_not(first))
    def _():
        greet(prv[0])
        greet(prv[1])

    own_prompt = [
        pltpu.make_async_copy(src.at[pl.ds(k * 4, 4)], pkv.at[:, i, 0, 0], sem_small.at[i])
        for i, src in enumerate((pk_hbm, pv_hbm))
    ]
    for copy in own_prompt:
        copy.start()
    small = [
        pltpu.make_async_copy(ids_hbm, ids, sem_small.at[2]),
        pltpu.make_async_copy(pat_hbm, pat, sem_small.at[3]),
    ]
    for copy in small:
        copy.start()

    def own_parts(h):
        return [
            pltpu.make_async_copy(q_hbm.at[:, cols(k, h, 512)], qb.at[h, rows], sem_in.at[h, 0]),
            pltpu.make_async_copy(u_hbm.at[:, cols(k, h, 512)], ub.at[h, rows], sem_in.at[h, 1]),
            pltpu.make_async_copy(k_hbm.at[:, cols(k, h, 128)], kw.at[h, own_rows], sem_in.at[h, 2]),
            pltpu.make_async_copy(v_hbm.at[:, cols(k, h, 128)], vw.at[h, own_rows], sem_in.at[h, 3]),
        ]

    for h in range(4):
        for copy in own_parts(h):
            copy.start()

    others = 4 + 6 * jnp.where((zl == 0) | (zl == 3), 1, 0) + 2 * jnp.where(first, 0, 1) + 2 * jnp.where(last, 0, 1)
    pl.semaphore_wait(barrier, others)

    def part_own(d):
        return send(pkv.at[:, :, 0, 0], pkv.at[:, :, 4 - d, 0], snd_own.at[d], rcv_own.at[d], y_peer[d])

    def part_z(h, j, slot, where):
        return send(pkv.at[h, :, 0, 0], pkv.at[h, :, 0, slot], snd_z.at[h, j], rcv_z.at[h, slot], where)

    def parts_z(h, way):
        return [part_z(h, j, slot, along_z(d, to_zl)) for j, (slot, d, to_zl) in enumerate(way)]

    def part_c(h, d):
        src, dst = pkv.at[h, :, 0, 1:4], pkv.at[h, :, 4 - d, 1:4]
        return send(src, dst, snd_c.at[h, d], rcv_c.at[h, d], y_peer[d])

    turn = (2, 1, 3)

    for copy in own_prompt:
        copy.wait()
    for at, way in ((3, upwards), (0, downwards)):

        @pl.when(zl == at)
        def _(way=way):
            for h in range(4):
                for copy in parts_z(h, way):
                    copy.start()

    for d in turn:
        part_own(d).start()

    def to_sib(h):
        far = 1 - k
        return [
            send(q_hbm.at[:, cols(far, h, 512)], qb.at[h, rows], snd_sib.at[h, 0], rcv_sib.at[h, 0], sib),
            send(u_hbm.at[:, cols(far, h, 512)], ub.at[h, rows], snd_sib.at[h, 1], rcv_sib.at[h, 1], sib),
            send(k_hbm.at[:, cols(far, h, 128)], kw.at[h, own_rows], snd_sib.at[h, 2], rcv_sib.at[h, 2], sib),
            send(v_hbm.at[:, cols(far, h, 128)], vw.at[h, own_rows], snd_sib.at[h, 3], rcv_sib.at[h, 3], sib),
        ]

    def halo(h, core, i):
        src, dst = ((k_hbm, kw), (v_hbm, vw))[i]
        return send(
            src.at[:, cols(core, h, 128)], dst.at[h, rows], snd_halo.at[h, core, i], rcv_halo.at[h, k, i], nxt[core]
        )

    for h in range(4):
        for copy in to_sib(h):
            copy.start()

    def halos():
        for h in range(4):
            for core in range(2):
                for i in range(2):
                    halo(h, core, i).start()

    pl.when(x < 3)(halos)

    @pl.when(first)
    def _():
        kw[:, 0:256] = jnp.zeros((4, 256, HD), BF)
        vw[:, 0:256] = jnp.zeros((4, 256, HD), BF)

    @pl.when(last)
    def _():
        gnext[...] = jnp.zeros((8, 2, BLK, HD), BF)

    for copy in small:
        copy.wait()
    base = jnp.maximum(c - 1, 0) * 256
    id_rows = [
        ids[:, pl.ds(pl.multiple_of(base + b * BLK, BLK), BLK)].astype(F32) for b in range(2)
    ] + [ids[:, pl.ds(pl.multiple_of(c * 256 + b * BLK, BLK), BLK)].astype(F32) for b in range(2)]
    wide = [jnp.broadcast_to(r, (BLK, BLK)) for r in id_rows]
    tall = [w.T for w in wide]
    key_at = lax.broadcasted_iota(jnp.int32, (BLK, BLK), 0)
    row_at = lax.broadcasted_iota(jnp.int32, (BLK, BLK), 1)
    inside = jnp.where(first, 0, 1)
    for rb in range(2):
        at = 2 * c + rb
        for t in range(3):
            b = rb + t
            seen = tall[b] == wide[2 + rb]
            if t == 2:
                seen = seen & (key_at <= row_at)
            else:
                flag = pat[0, at, jnp.maximum(at - 2 + t, 0)]
                if b < 2:
                    flag = flag * inside
                seen = seen & (jnp.full((BLK, BLK), flag, jnp.int32) > 0)
            bias[rb, t * BLK : (t + 1) * BLK] = jnp.where(seen, 0.0, HIDE)

    def along_y(h):
        for slot in (1, 3, 2):
            part_z(h, 0, slot, source[slot]).wait_recv()
        for d in turn:
            part_c(h, d).start()

    along_y(0)
    pl.when((x == 3) & jnp.logical_not(last))(halos)
    along_y(1)
    for d in turn:
        part_own(d).wait_recv()

    def to_prev(h, core):
        part = gs.at[h, :, core * BLK : (core + 1) * BLK]
        return send(part, gnext.at[k * 4 + h], snd_gprev.at[h, core], rcv_gnext.at[k * 4 + h], prv[core])

    def grads_to_sib(h):
        return send(gs.at[h, :, sib_rows], gown.at[k * 4 + h], snd_gsib.at[h], rcv_gsib.at[h], sib)

    def gq_own(h):
        return pltpu.make_async_copy(gqb.at[h, rows], gq_hbm.at[:, cols(k, h, 512)], sem_gq.at[h])

    def gq_to_sib(h):
        return send(gqb.at[h, other], gq_hbm.at[:, cols(k, h, 512)], snd_gq.at[h], rcv_gq.at[h], sib)

    @pl.loop(0, 4)
    def _(h):
        @pl.when(h < 2)
        def _():
            along_y(h + 2)

        for copy in own_parts(h):
            copy.wait()
        for copy in to_sib(h):
            copy.wait_recv()
        for d in turn:
            part_c(h, d).wait_recv()

        @pl.when(jnp.logical_not(first))
        def _():
            for core in range(2):
                for i in range(2):
                    dst = (kw, vw)[i].at[h, core * BLK : (core + 1) * BLK]
                    send(dst, dst, snd_halo.at[h, core, i], rcv_halo.at[h, core, i], prv[0]).wait_recv()

        pk = pkv[h, 0].reshape(512, HD)
        pv = pkv[h, 1].reshape(512, HD)
        pk_t = pk.T
        kw_t = kw[h].T

        def half(rb):
            qr = qb[h, rb * BLK : (rb + 1) * BLK]
            ur = ub[h, rb * BLK : (rb + 1) * BLK]
            q = jnp.concatenate([qr[:, g * HD : (g + 1) * HD] for g in range(4)], 0)
            u = jnp.concatenate([ur[:, g * HD : (g + 1) * HD] for g in range(4)], 0)
            near = slice(rb * BLK, rb * BLK + 384)
            gq, gk, gv = tile_grads(q, u, pk, pv, kw[h, near], vw[h, near], bias[rb], pk_t, kw_t[:, near])
            for g in range(4):
                gqb[h, rb * BLK : (rb + 1) * BLK, g * HD : (g + 1) * HD] = gq[g * BLK : (g + 1) * BLK].astype(BF)
            return gk, gv

        a = half(0)
        for i in range(2):
            gs[h, i, 0:128] = a[i][0:128].astype(BF)
            acc[i] = a[i][128:384]
        pl.when(jnp.logical_not(first))(to_prev(h, 0).start)
        b = half(1)
        for i in range(2):
            gs[h, i, 128:384] = (acc[i] + b[i][0:256]).astype(BF)
            gs[h, i, 384:512] = b[i][256:384].astype(BF)
        pl.when(jnp.logical_not(first))(to_prev(h, 1).start)

        grads_to_sib(h).start()
        gq_to_sib(h).start()
        gq_own(h).start()
        gown[k * 4 + h] = gs[h, :, own_rows]

    def outs(hh):
        return [
            pltpu.make_async_copy(fin.at[hh, i], out.at[:, hh * HD : (hh + 1) * HD], sem_out.at[hh, i])
            for i, out in enumerate((gk_hbm, gv_hbm))
        ]

    for h in range(4):
        send(gs.at[h, :, sib_rows], gown.at[(1 - k) * 4 + h], snd_gsib.at[h], rcv_gsib.at[h], sib).wait_recv()
        for core in range(2):

            @pl.when(jnp.logical_not(last))
            def _(core=core, h=h):
                part = gnext.at[core * 4 + h]
                send(part, part, snd_gprev.at[h, core], rcv_gnext.at[core * 4 + h], nxt[0]).wait_recv()

            hh = core * 4 + h
            fin[hh] = (gown[hh].astype(F32) + gnext[hh].astype(F32)).astype(BF)
            for copy in outs(hh):
                copy.start()

    for h in range(4):
        gq_own(h).wait()
        copy = gq_to_sib(h)
        copy.wait_send()
        send(gqb.at[h, rows], gq_hbm.at[:, cols(1 - k, h, 512)], snd_gq.at[h], rcv_gq.at[h], sib).wait_recv()
        grads_to_sib(h).wait_send()
        for copy in to_sib(h):
            copy.wait_send()
        for d in (1, 2, 3):
            part_c(h, d).wait_send()

    for d in turn:
        part_own(d).wait_send()
    for at, way in ((3, upwards), (0, downwards)):

        @pl.when(zl == at)
        def _(way=way):
            for h in range(4):
                for copy in parts_z(h, way):
                    copy.wait_send()

    @pl.when(jnp.logical_not(last))
    def _():
        for h in range(4):
            for core in range(2):
                for i in range(2):
                    halo(h, core, i).wait_send()

    @pl.when(jnp.logical_not(first))
    def _():
        for h in range(4):
            for core in range(2):
                to_prev(h, core).wait_send()

    for hh in range(KVH):
        for copy in outs(hh):
            copy.wait()


def shards(queries, keys, values, cotangent, prompt_keys, prompt_values, response_ids, block_pattern):
    anywhere = pl.BlockSpec(memory_space=pl.ANY)
    dma = pltpu.SemaphoreType.DMA
    return pl.pallas_call(
        kernel,
        out_shape=[
            jax.ShapeDtypeStruct(queries.shape, BF),
            jax.ShapeDtypeStruct(keys.shape, BF),
            jax.ShapeDtypeStruct(values.shape, BF),
        ],
        in_specs=[anywhere] * 8,
        out_specs=[anywhere] * 3,
        scratch_shapes=[
            pltpu.VMEM((1, 4096), jnp.int32),
            pltpu.SMEM((1, 32, 32), jnp.int32),
            pltpu.VMEM((2, 384, BLK), F32),
            pltpu.VMEM((4, 256, 512), BF),
            pltpu.VMEM((4, 256, 512), BF),
            pltpu.VMEM((4, 512, HD), BF),
            pltpu.VMEM((4, 512, HD), BF),
            pltpu.VMEM((4, 2, 4, 4, 32, HD), BF),
            pltpu.VMEM((4, 2, 512, HD), BF),
            pltpu.VMEM((8, 2, BLK, HD), BF),
            pltpu.VMEM((8, 2, BLK, HD), BF),
            pltpu.VMEM((4, 256, 512), BF),
            pltpu.VMEM((8, 2, BLK, HD), BF),
            pltpu.VMEM((2, 256, HD), F32),
            dma((4, 4)), dma((4,)), dma((1,)),
            dma((4,)), dma((4,)), dma((4, 6)), dma((4, 4)), dma((4, 4)), dma((4, 4)),
            dma((4, 4)), dma((4, 4)), dma((4, 2, 2)), dma((4, 2, 2)), dma((4,)), dma((4,)), dma((4,)),
            dma((4,)), dma((4,)), dma((4, 2)), dma((8,)), dma((8, 2)),
        ],
        compiler_params=pltpu.CompilerParams(
            collective_id=0, has_side_effects=True, vmem_limit_bytes=60 << 20
        ),
        cost_estimate=pl.CostEstimate(flops=4 << 30, bytes_accessed=8 << 20, transcendentals=4 << 20),
        name="tree_attention_backward",
    )(queries, cotangent, keys, values, prompt_keys, prompt_values, response_ids, block_pattern)


def solution(mesh):
    tokens = P(("sample", "head"), None)
    prompt = P(None, "sample", None)
    return jax.shard_map(
        shards,
        mesh=mesh,
        in_specs=(tokens, tokens, tokens, tokens, prompt, prompt, P("sample", None), P("sample", None, None)),
        out_specs=(tokens, tokens, tokens),
        check_vma=False,
    )
```

```python
import math

import jax
import jax.numpy as jnp
from jax import lax
from jax.experimental import pallas as pl
from jax.experimental.pallas import tpu as pltpu
from jax.sharding import PartitionSpec as P

KVH = 8
HD = 128
BLK = 128
SCALE = HD**-0.5
SCALE2 = SCALE * math.log2(math.e)
HIDE = -1e30
MESH = pl.DeviceIdType.MESH
BF = jnp.bfloat16
F32 = jnp.float32

NT = (((1,), (1,)), ((), ()))
NN = (((1,), (0,)), ((), ()))


def dot(a, b, dims):
    return lax.dot_general(a, b, dims, preferred_element_type=F32)


def spread(rows):
    return jnp.concatenate([rows[:, g * HD : (g + 1) * HD] for g in range(4)], 0)


def causal_block():
    keys = lax.broadcasted_iota(jnp.int32, (BLK, BLK), 0)
    at = lax.broadcasted_iota(jnp.int32, (BLK, BLK), 1)
    return keys <= at


def window_scores(q, u, kw, vw, bias, causal):
    def products(a, b):
        first, middle, last = [dot(a[i * BLK : (i + 1) * BLK], b, NT) for i in range(3)]
        return jnp.concatenate([middle, jnp.where(causal, last, first)], 0)

    sw = products(kw, q) * SCALE2 + bias
    return sw, products(vw, u), jnp.max(sw, 0, keepdims=True)


def unfold(both, causal):
    middle, shared = both[:BLK], both[BLK:]
    zero = jnp.zeros_like(shared)
    return jnp.concatenate([jnp.where(causal, zero, shared), middle, jnp.where(causal, shared, zero)], 0)


class Tile:
    def __init__(self, q, u, pk, pv, pk_t, kw_t, sw, dw, top):
        self.q, self.u, self.pk, self.pv, self.pk_t, self.kw_t = q, u, pk, pv, pk_t, kw_t
        self.sw, self.dw, self.peak = sw, dw, top
        self.sp, self.dp, self.ep, self.ds = [], [], [], []

    def scores(self, j):
        part = slice(j * BLK, (j + 1) * BLK)
        self.sp.append(dot(self.pk[part], self.q, NT))
        self.dp.append(dot(self.pv[part], self.u, NT))
        self.peak = jnp.maximum(self.peak, jnp.max(self.sp[j], 0, keepdims=True) * SCALE2)

    def begin(self):
        self.ew = jnp.exp2(self.sw[...] - self.peak)
        self.total = jnp.sum(self.ew, 0, keepdims=True)
        self.center = jnp.sum(self.ew * self.dw[...], 0, keepdims=True)

    def expo(self, j):
        e = jnp.exp2(self.sp[j] * SCALE2 - self.peak)
        self.ep.append(e)
        self.total = self.total + jnp.sum(e, 0, keepdims=True)
        self.center = self.center + jnp.sum(e * self.dp[j], 0, keepdims=True)

    def window(self, causal):
        self.inv = 1.0 / self.total
        self.center = self.center * self.inv
        w = self.ew * self.inv
        dsw = ((w * SCALE) * (self.dw[...] - self.center)).astype(BF)
        self.dsw = unfold(dsw, causal)
        return dot(self.dsw, self.q, NN), dot(unfold(w.astype(BF), causal), self.u, NN)

    def dscores(self, j):
        self.ds.append(((self.ep[j] * (self.inv * SCALE)) * (self.dp[j] - self.center)).astype(BF))

    def grad_queries(self):
        keys = jnp.concatenate([self.pk_t, self.kw_t], 1)
        return dot(keys, jnp.concatenate(self.ds + [self.dsw], 0), NN).astype(BF).T


def kernel(
    q_hbm, u_hbm, k_hbm, v_hbm, pk_hbm, pv_hbm, ids_hbm, pat_hbm,
    gq_hbm, gk_hbm, gv_hbm,
    ids, pat, bias, qb, ub, kw, vw, pkv, gs, gown, gnext, gqb, fin, sbuf, dbuf, top,
    sem_in, sem_small, sem_own,
    snd_own, rcv_own, snd_z, rcv_z, snd_c, rcv_c,
    snd_sib, rcv_sib, snd_halo, rcv_halo, snd_gq, rcv_gq, sem_gq,
    snd_gsib, rcv_gsib, snd_gprev, rcv_gnext, sem_out,
):
    s = lax.axis_index("sample")
    hd = lax.axis_index("head")
    y, zh = s // 4, s % 4
    c, k = hd // 2, hd % 2
    zl, x = hd // 8, c % 4
    first, last = c == 0, c == 15
    sib = (s, c * 2 + (1 - k))
    nxt = [(s, jnp.minimum(c + 1, 15) * 2 + i) for i in range(2)]
    prv = [(s, jnp.maximum(c - 1, 0) * 2 + i) for i in range(2)]
    column = lax.rem(hd, 8)

    def along_z(d, to_zl):
        return (y * 4 + lax.rem(zh + d, 4), to_zl * 8 + column)

    y_peer = [(lax.rem(y + d, 4) * 4 + zh, hd) for d in range(4)]
    rows = pl.ds(pl.multiple_of(k * BLK, BLK), BLK)
    other = pl.ds(pl.multiple_of((1 - k) * BLK, BLK), BLK)
    own_rows = pl.ds(pl.multiple_of(256 + k * BLK, BLK), BLK)
    sib_rows = pl.ds(pl.multiple_of(256 + (1 - k) * BLK, BLK), BLK)

    def cols(core, h, width):
        return pl.ds(pl.multiple_of((core * 4 + h) * width, BLK), width)

    def send(src, dst, snd, rcv, where):
        return pltpu.make_async_remote_copy(
            src_ref=src, dst_ref=dst, send_sem=snd, recv_sem=rcv, device_id=where, device_id_type=MESH
        )

    barrier = pltpu.get_barrier_semaphore()

    def greet(where):
        pl.semaphore_signal(barrier, inc=1, device_id=where, device_id_type=MESH)

    upwards = [(3, 2, 1), (3, 2, 0), (2, 1, 3), (2, 1, 2), (2, 1, 1), (2, 1, 0)]
    downwards = [(3, 2, 2), (3, 2, 3), (1, 3, 0), (1, 3, 1), (1, 3, 2), (1, 3, 3)]
    source = {1: along_z(1, 0), 2: along_z(3, 3), 3: along_z(2, jnp.where(zl < 2, 3, 0))}
    for where in [sib] + y_peer[1:] + list(source.values()):
        greet(where)

    @pl.when(jnp.logical_not(last))
    def _():
        greet(nxt[0])
        greet(nxt[1])

    @pl.when(jnp.logical_not(first))
    def _():
        greet(prv[0])
        greet(prv[1])

    own_prompt = [
        pltpu.make_async_copy(src.at[pl.ds(k * 4, 4)], pkv.at[:, i, 0, 0], sem_small.at[i])
        for i, src in enumerate((pk_hbm, pv_hbm))
    ]
    for copy in own_prompt:
        copy.start()
    small = [
        pltpu.make_async_copy(ids_hbm, ids, sem_small.at[2]),
        pltpu.make_async_copy(pat_hbm, pat, sem_small.at[3]),
    ]
    for copy in small:
        copy.start()

    def own_parts(h):
        return [
            pltpu.make_async_copy(q_hbm.at[:, cols(k, h, 512)], qb.at[h, rows], sem_in.at[h, 0]),
            pltpu.make_async_copy(u_hbm.at[:, cols(k, h, 512)], ub.at[h, rows], sem_in.at[h, 1]),
            pltpu.make_async_copy(k_hbm.at[:, cols(k, h, 128)], kw.at[h, own_rows], sem_in.at[h, 2]),
            pltpu.make_async_copy(v_hbm.at[:, cols(k, h, 128)], vw.at[h, own_rows], sem_in.at[h, 3]),
        ]

    for h in range(4):
        for copy in own_parts(h):
            copy.start()

    others = 4 + 6 * jnp.where((zl == 0) | (zl == 3), 1, 0) + 2 * jnp.where(first, 0, 1) + 2 * jnp.where(last, 0, 1)
    pl.semaphore_wait(barrier, others)

    def part_own(d):
        return send(pkv.at[:, :, 0, 0], pkv.at[:, :, 4 - d, 0], snd_own.at[d], rcv_own.at[d], y_peer[d])

    def part_z(h, j, slot, where):
        return send(pkv.at[h, :, 0, 0], pkv.at[h, :, 0, slot], snd_z.at[h, j], rcv_z.at[h, slot], where)

    def parts_z(h, way):
        return [part_z(h, j, slot, along_z(d, to_zl)) for j, (slot, d, to_zl) in enumerate(way)]

    def part_c(h, d, far):
        sub = slice(3, 4) if far else slice(1, 3)
        src, dst = pkv.at[h, :, 0, sub], pkv.at[h, :, 4 - d, sub]
        return send(src, dst, snd_c.at[far, h, d], rcv_c.at[far, h, d], y_peer[d])

    turn = (2, 1, 3)

    for copy in own_prompt:
        copy.wait()
    for at, way in ((3, upwards), (0, downwards)):

        @pl.when(zl == at)
        def _(way=way):
            for h in range(4):
                for copy in parts_z(h, way):
                    copy.start()

    for d in turn:
        part_own(d).start()

    def to_sib(h):
        far = 1 - k
        return [
            send(q_hbm.at[:, cols(far, h, 512)], qb.at[h, rows], snd_sib.at[h, 0], rcv_sib.at[h, 0], sib),
            send(u_hbm.at[:, cols(far, h, 512)], ub.at[h, rows], snd_sib.at[h, 1], rcv_sib.at[h, 1], sib),
            send(k_hbm.at[:, cols(far, h, 128)], kw.at[h, own_rows], snd_sib.at[h, 2], rcv_sib.at[h, 2], sib),
            send(v_hbm.at[:, cols(far, h, 128)], vw.at[h, own_rows], snd_sib.at[h, 3], rcv_sib.at[h, 3], sib),
        ]

    def halo(h, core, i):
        src, dst = ((k_hbm, kw), (v_hbm, vw))[i]
        return send(
            src.at[:, cols(core, h, 128)], dst.at[h, rows], snd_halo.at[h, core, i], rcv_halo.at[h, k, i], nxt[core]
        )

    for h in range(4):
        for copy in to_sib(h):
            copy.start()

    def halos():
        for h in range(4):
            for core in range(2):
                for i in range(2):
                    halo(h, core, i).start()

    pl.when(x < 3)(halos)

    @pl.when(first)
    def _():
        kw[:, 0:256] = jnp.zeros((4, 256, HD), BF)
        vw[:, 0:256] = jnp.zeros((4, 256, HD), BF)

    @pl.when(last)
    def _():
        gnext[...] = jnp.zeros((8, 2, BLK, HD), BF)

    for copy in small:
        copy.wait()
    base = jnp.maximum(c - 1, 0) * 256
    id_rows = [
        ids[:, pl.ds(pl.multiple_of(base + b * BLK, BLK), BLK)].astype(F32) for b in range(2)
    ] + [ids[:, pl.ds(pl.multiple_of(c * 256 + b * BLK, BLK), BLK)].astype(F32) for b in range(2)]
    wide = [jnp.broadcast_to(r, (BLK, BLK)) for r in id_rows]
    tall = [w.T for w in wide]
    causal1 = causal_block()
    causal = jnp.concatenate([causal1] * 4, 1)
    inside = jnp.where(first, 0, 1)
    for rb in range(2):
        at = 2 * c + rb

        def earlier(step, rb=rb, at=at):
            b = rb + 2 - step
            flag = pat[0, at, jnp.maximum(at - step, 0)]
            if b < 2:
                flag = flag * inside
            return (tall[b] == wide[2 + rb]) & (jnp.full((BLK, BLK), flag, jnp.int32) > 0)

        own = tall[2 + rb] == wide[2 + rb]
        shared = (causal1 & own) | (jnp.logical_not(causal1) & earlier(2))
        for i, seen in enumerate((earlier(1), shared)):
            part = jnp.where(seen, 0.0, HIDE)
            bias[rb, i * BLK : (i + 1) * BLK] = jnp.concatenate([part] * 4, 1)

    def along_y(h, between=None):
        for slot in (1, 2):
            part_z(h, 0, slot, source[slot]).wait_recv()
        for d in turn:
            part_c(h, d, 0).start()
        if between is not None:
            between()
        part_z(h, 0, 3, source[3]).wait_recv()
        for d in turn:
            part_c(h, d, 1).start()

    def late_halos(h):
        pl.when((h == 0) & (x == 3) & jnp.logical_not(last))(halos)

    def window_part(h):
        for copy in own_parts(h):
            copy.wait()
        for copy in to_sib(h):
            copy.wait_recv()

        @pl.when(jnp.logical_not(first))
        def _():
            for core in range(2):
                for i in range(2):
                    dst = (kw, vw)[i].at[h, core * BLK : (core + 1) * BLK]
                    send(dst, dst, snd_halo.at[h, core, i], rcv_halo.at[h, core, i], prv[0]).wait_recv()

        for rb in range(2):
            q = spread(qb[h, rb * BLK : (rb + 1) * BLK])
            u = spread(ub[h, rb * BLK : (rb + 1) * BLK])
            near = slice(rb * BLK, rb * BLK + 384)
            sbuf[h, rb], dbuf[h, rb], top[h, rb] = window_scores(q, u, kw[h, near], vw[h, near], bias[rb], causal)

    early = (x > 0) | first

    @pl.loop(0, 4)
    def _(h):
        pl.when(early)(lambda: window_part(h))

        @pl.when(h < 3)
        def _():
            along_y(h, lambda: late_halos(h))

    for d in turn:
        part_own(d).wait_recv()

    def to_prev(h, core):
        part = gs.at[h, :, core * BLK : (core + 1) * BLK]
        return send(part, gnext.at[k * 4 + h], snd_gprev.at[h, core], rcv_gnext.at[k * 4 + h], prv[core])

    def grads_to_sib(h):
        return send(gs.at[h, :, sib_rows], gown.at[k * 4 + h], snd_gsib.at[h], rcv_gsib.at[h], sib)

    def gq_own(h):
        return pltpu.make_async_copy(gqb.at[h, rows], gq_hbm.at[:, cols(k, h, 512)], sem_gq.at[h])

    def gq_to_sib(h):
        return send(gqb.at[h, other], gq_hbm.at[:, cols(k, h, 512)], snd_gq.at[h], rcv_gq.at[h], sib)

    @pl.loop(0, 4)
    def _(h):
        @pl.when(h == 1)
        def _():
            along_y(3)

        pl.when(jnp.logical_not(early))(lambda: window_part(h))
        for d in turn:
            for far in range(2):
                part_c(h, d, far).wait_recv()

        pk = pkv[h, 0].reshape(512, HD)
        pv = pkv[h, 1].reshape(512, HD)
        pk_t = pk.T
        kw_t = kw[h].T

        a, b = [
            Tile(
                spread(qb[h, rb * BLK : (rb + 1) * BLK]),
                spread(ub[h, rb * BLK : (rb + 1) * BLK]),
                pk, pv, pk_t, kw_t[:, rb * BLK : rb * BLK + 384],
                sbuf.at[h, rb], dbuf.at[h, rb], top[h, rb],
            )
            for rb in range(2)
        ]

        def store_gq(rb, gq):
            for g in range(4):
                gqb[h, rb * BLK : (rb + 1) * BLK, g * HD : (g + 1) * HD] = gq[g * BLK : (g + 1) * BLK]

        for j in range(4):
            a.scores(j)
        a.begin()
        for j in range(4):
            b.scores(j)
            a.expo(j)
        grads_a = a.window(causal)
        b.begin()
        for j in range(4):
            b.expo(j)
        grads_b = b.window(causal)
        for i in range(2):
            gs[h, i, 0:128] = grads_a[i][0:128].astype(BF)
            gs[h, i, 128:384] = (grads_a[i][128:384] + grads_b[i][0:256]).astype(BF)
            gs[h, i, 384:512] = grads_b[i][256:384].astype(BF)

        @pl.when(jnp.logical_not(first))
        def _():
            to_prev(h, 0).start()
            to_prev(h, 1).start()

        for rb, tile in enumerate((a, b)):
            for j in range(4):
                tile.dscores(j)
            store_gq(rb, tile.grad_queries())

        grads_to_sib(h).start()
        gq_to_sib(h).start()
        gq_own(h).start()
        gown[k * 4 + h] = gs[h, :, own_rows]

    def outs(hh):
        return [
            pltpu.make_async_copy(fin.at[hh, i], out.at[:, hh * HD : (hh + 1) * HD], sem_out.at[hh, i])
            for i, out in enumerate((gk_hbm, gv_hbm))
        ]

    for h in range(4):
        send(gs.at[h, :, sib_rows], gown.at[(1 - k) * 4 + h], snd_gsib.at[h], rcv_gsib.at[h], sib).wait_recv()
        for core in range(2):

            @pl.when(jnp.logical_not(last))
            def _(core=core, h=h):
                part = gnext.at[core * 4 + h]
                send(part, part, snd_gprev.at[h, core], rcv_gnext.at[core * 4 + h], nxt[0]).wait_recv()

            hh = core * 4 + h
            fin[hh] = (gown[hh].astype(F32) + gnext[hh].astype(F32)).astype(BF)
            for copy in outs(hh):
                copy.start()

    for h in range(4):
        gq_own(h).wait()
        copy = gq_to_sib(h)
        copy.wait_send()
        send(gqb.at[h, rows], gq_hbm.at[:, cols(1 - k, h, 512)], snd_gq.at[h], rcv_gq.at[h], sib).wait_recv()
        grads_to_sib(h).wait_send()
        for copy in to_sib(h):
            copy.wait_send()
        for d in (1, 2, 3):
            for far in range(2):
                part_c(h, d, far).wait_send()

    for d in turn:
        part_own(d).wait_send()
    for at, way in ((3, upwards), (0, downwards)):

        @pl.when(zl == at)
        def _(way=way):
            for h in range(4):
                for copy in parts_z(h, way):
                    copy.wait_send()

    @pl.when(jnp.logical_not(last))
    def _():
        for h in range(4):
            for core in range(2):
                for i in range(2):
                    halo(h, core, i).wait_send()

    @pl.when(jnp.logical_not(first))
    def _():
        for h in range(4):
            for core in range(2):
                to_prev(h, core).wait_send()

    for hh in range(KVH):
        for copy in outs(hh):
            copy.wait()


def hand_over(gq, gk, gv, gq_out, gk_out, gv_out, gq_at, gk_at, gv_at, sem_in, sem_out):
    parts = [(ref, slice(0, BLK)) for ref in ((gk, gk_at, gk_out), (gv, gv_at, gv_out))]
    parts += [((gq, gq_at, gq_out), slice(i * 32, (i + 1) * 32)) for i in range(4)]
    loads, stores = [], []
    for i, ((src, at, out), part) in enumerate(parts):
        loads.append(pltpu.make_async_copy(src.at[part], at.at[part], sem_in.at[i]))
        stores.append(pltpu.make_async_copy(at.at[part], out.at[part], sem_out.at[i]))
    for copy in loads:
        copy.start()
    for load, store in zip(loads, stores):
        load.wait()
        store.start()
    for copy in stores:
        copy.wait()


def shards(queries, keys, values, cotangent, prompt_keys, prompt_values, response_ids, block_pattern):
    anywhere = pl.BlockSpec(memory_space=pl.ANY)
    dma = pltpu.SemaphoreType.DMA
    shapes = [jax.ShapeDtypeStruct(a.shape, BF) for a in (queries, keys, values)]
    grads = pl.pallas_call(
        kernel,
        out_shape=shapes,
        in_specs=[anywhere] * 8,
        out_specs=[anywhere] * 3,
        scratch_shapes=[
            pltpu.VMEM((1, 4096), jnp.int32),
            pltpu.SMEM((1, 32, 32), jnp.int32),
            pltpu.VMEM((2, 256, 512), F32),
            pltpu.VMEM((4, 256, 512), BF),
            pltpu.VMEM((4, 256, 512), BF),
            pltpu.VMEM((4, 512, HD), BF),
            pltpu.VMEM((4, 512, HD), BF),
            pltpu.VMEM((4, 2, 4, 4, 32, HD), BF),
            pltpu.VMEM((4, 2, 512, HD), BF),
            pltpu.VMEM((8, 2, BLK, HD), BF),
            pltpu.VMEM((8, 2, BLK, HD), BF),
            pltpu.VMEM((4, 256, 512), BF),
            pltpu.VMEM((8, 2, BLK, HD), BF),
            pltpu.VMEM((4, 2, 256, 512), F32),
            pltpu.VMEM((4, 2, 256, 512), F32),
            pltpu.VMEM((4, 2, 1, 512), F32),
            dma((4, 4)), dma((4,)), dma((1,)),
            dma((4,)), dma((4,)), dma((4, 6)), dma((4, 4)), dma((2, 4, 4)), dma((2, 4, 4)),
            dma((4, 4)), dma((4, 4)), dma((4, 2, 2)), dma((4, 2, 2)), dma((4,)), dma((4,)), dma((4,)),
            dma((4,)), dma((4,)), dma((4, 2)), dma((8,)), dma((8, 2)),
        ],
        compiler_params=pltpu.CompilerParams(
            collective_id=0, has_side_effects=True, vmem_limit_bytes=60 << 20
        ),
        cost_estimate=pl.CostEstimate(flops=4 << 30, bytes_accessed=8 << 20, transcendentals=4 << 20),
        name="tree_attention_backward",
    )(queries, cotangent, keys, values, prompt_keys, prompt_values, response_ids, block_pattern)
    return pl.pallas_call(
        hand_over,
        out_shape=shapes,
        in_specs=[anywhere] * 3,
        out_specs=[anywhere] * 3,
        scratch_shapes=[pltpu.VMEM(a.shape, BF) for a in shapes] + [dma((6,)), dma((6,))],
        compiler_params=pltpu.CompilerParams(vmem_limit_bytes=60 << 20),
        name="hand_over",
    )(*grads)


def solution(mesh):
    tokens = P(("sample", "head"), None)
    prompt = P(None, "sample", None)
    return jax.shard_map(
        shards,
        mesh=mesh,
        in_specs=(tokens, tokens, tokens, tokens, prompt, prompt, P("sample", None), P("sample", None, None)),
        out_specs=(tokens, tokens, tokens),
        check_vma=False,
    )
```

```python
import math

import jax
import jax.numpy as jnp
from jax import lax
from jax.experimental import pallas as pl
from jax.experimental.pallas import tpu as pltpu
from jax.sharding import PartitionSpec as P

KVH = 8
HD = 128
BLK = 128
SCALE = HD**-0.5
SCALE2 = SCALE * math.log2(math.e)
HIDE = -1e30
MESH = pl.DeviceIdType.MESH
BF = jnp.bfloat16
F32 = jnp.float32

NT = (((1,), (1,)), ((), ()))
NN = (((1,), (0,)), ((), ()))


def dot(a, b, dims):
    return lax.dot_general(a, b, dims, preferred_element_type=F32)


def spread(rows):
    return jnp.concatenate([rows[:, g * HD : (g + 1) * HD] for g in range(4)], 0)


def causal_block():
    keys = lax.broadcasted_iota(jnp.int32, (BLK, BLK), 0)
    at = lax.broadcasted_iota(jnp.int32, (BLK, BLK), 1)
    return keys <= at


def window_scores(q, u, kw, vw, bias, causal):
    def products(a, b):
        out = dot(a, b, NT)
        return jnp.concatenate([out[BLK : 2 * BLK], jnp.where(causal, out[2 * BLK :], out[:BLK])], 0)

    sw = products(kw, q) * SCALE2 + bias
    return sw, products(vw, u), jnp.max(sw, 0, keepdims=True)


def unfold(both, causal):
    middle, shared = both[:BLK], both[BLK:]
    zero = jnp.zeros_like(shared)
    return jnp.concatenate([jnp.where(causal, zero, shared), middle, jnp.where(causal, shared, zero)], 0)


class Tile:
    def __init__(self, q, u, pk, pv, pk_t, kw_t, sw, dw, top):
        self.q, self.u, self.pk, self.pv, self.pk_t, self.kw_t = q, u, pk, pv, pk_t, kw_t
        self.sw, self.dw, self.peak = sw, dw, top

    def scores(self):
        self.sp = dot(self.pk, self.q, NT)
        self.peak = jnp.maximum(self.peak, jnp.max(self.sp, 0, keepdims=True) * SCALE2)
        self.dp = dot(self.pv, self.u, NT)

    def expo(self):
        self.ew = jnp.exp2(self.sw[...] - self.peak)
        self.ep = jnp.exp2(self.sp * SCALE2 - self.peak)
        total = jnp.sum(self.ew, 0, keepdims=True) + jnp.sum(self.ep, 0, keepdims=True)
        center = jnp.sum(self.ew * self.dw[...], 0, keepdims=True) + jnp.sum(self.ep * self.dp, 0, keepdims=True)
        self.inv = 1.0 / total
        self.center = center * self.inv

    def window(self, causal):
        w = self.ew * self.inv
        dsw = ((w * SCALE) * (self.dw[...] - self.center)).astype(BF)
        self.dsw = unfold(dsw, causal)
        return dot(self.dsw, self.q, NN), dot(unfold(w.astype(BF), causal), self.u, NN)

    def dscores(self):
        self.ds = (self.ep * (self.dp - self.center)).astype(BF)

    def grad_queries(self):
        prompt = dot(self.pk_t, self.ds, NN) * (self.inv * SCALE)
        return (prompt + dot(self.kw_t, self.dsw, NN)).astype(BF).T


def kernel(
    q_hbm, u_hbm, k_hbm, v_hbm, pk_hbm, pv_hbm, ids_hbm, pat_hbm,
    gq_hbm, gk_hbm, gv_hbm,
    ids, pat, bias, qb, ub, kw, vw, pkv, gs, gown, gnext, gqb, fin, sbuf, dbuf, top,
    sem_in, sem_small, sem_own,
    snd_own, rcv_own, snd_z, rcv_z, snd_c, rcv_c,
    snd_sib, rcv_sib, snd_halo, rcv_halo, snd_gq, rcv_gq, sem_gq,
    snd_gsib, rcv_gsib, snd_gprev, rcv_gnext, sem_out,
):
    s = lax.axis_index("sample")
    hd = lax.axis_index("head")
    y, zh = s // 4, s % 4
    c, k = hd // 2, hd % 2
    zl, x = hd // 8, c % 4
    first, last = c == 0, c == 15
    sib = (s, c * 2 + (1 - k))
    nxt = [(s, jnp.minimum(c + 1, 15) * 2 + i) for i in range(2)]
    prv = [(s, jnp.maximum(c - 1, 0) * 2 + i) for i in range(2)]
    column = lax.rem(hd, 8)

    def along_z(d, to_zl):
        return (y * 4 + lax.rem(zh + d, 4), to_zl * 8 + column)

    y_peer = [(lax.rem(y + d, 4) * 4 + zh, hd) for d in range(4)]
    rows = pl.ds(pl.multiple_of(k * BLK, BLK), BLK)
    other = pl.ds(pl.multiple_of((1 - k) * BLK, BLK), BLK)
    own_rows = pl.ds(pl.multiple_of(256 + k * BLK, BLK), BLK)
    sib_rows = pl.ds(pl.multiple_of(256 + (1 - k) * BLK, BLK), BLK)

    def cols(core, h, width):
        return pl.ds(pl.multiple_of((core * 4 + h) * width, BLK), width)

    def send(src, dst, snd, rcv, where):
        return pltpu.make_async_remote_copy(
            src_ref=src, dst_ref=dst, send_sem=snd, recv_sem=rcv, device_id=where, device_id_type=MESH
        )

    barrier = pltpu.get_barrier_semaphore()

    def greet(where):
        pl.semaphore_signal(barrier, inc=1, device_id=where, device_id_type=MESH)

    upwards = [(3, 2, 1), (3, 2, 0), (2, 1, 3), (2, 1, 2), (2, 1, 1), (2, 1, 0)]
    downwards = [(3, 2, 2), (3, 2, 3), (1, 3, 0), (1, 3, 1), (1, 3, 2), (1, 3, 3)]
    source = {1: along_z(1, 0), 2: along_z(3, 3), 3: along_z(2, jnp.where(zl < 2, 3, 0))}
    for where in [sib] + y_peer[1:] + list(source.values()):
        greet(where)

    @pl.when(jnp.logical_not(last))
    def _():
        greet(nxt[0])
        greet(nxt[1])

    @pl.when(jnp.logical_not(first))
    def _():
        greet(prv[0])
        greet(prv[1])

    own_prompt = [
        pltpu.make_async_copy(src.at[pl.ds(k * 4, 4)], pkv.at[:, i, 0, 0], sem_small.at[i])
        for i, src in enumerate((pk_hbm, pv_hbm))
    ]
    for copy in own_prompt:
        copy.start()
    small = [
        pltpu.make_async_copy(ids_hbm, ids, sem_small.at[2]),
        pltpu.make_async_copy(pat_hbm, pat, sem_small.at[3]),
    ]
    for copy in small:
        copy.start()

    def own_parts(h):
        return [
            pltpu.make_async_copy(q_hbm.at[:, cols(k, h, 512)], qb.at[h, rows], sem_in.at[h, 0]),
            pltpu.make_async_copy(u_hbm.at[:, cols(k, h, 512)], ub.at[h, rows], sem_in.at[h, 1]),
            pltpu.make_async_copy(k_hbm.at[:, cols(k, h, 128)], kw.at[h, own_rows], sem_in.at[h, 2]),
            pltpu.make_async_copy(v_hbm.at[:, cols(k, h, 128)], vw.at[h, own_rows], sem_in.at[h, 3]),
        ]

    for h in range(4):
        for copy in own_parts(h):
            copy.start()

    others = 4 + 6 * jnp.where((zl == 0) | (zl == 3), 1, 0) + 2 * jnp.where(first, 0, 1) + 2 * jnp.where(last, 0, 1)
    pl.semaphore_wait(barrier, others)

    def part_own(d):
        return send(pkv.at[:, :, 0, 0], pkv.at[:, :, 4 - d, 0], snd_own.at[d], rcv_own.at[d], y_peer[d])

    def part_z(h, j, slot, where):
        return send(pkv.at[h, :, 0, 0], pkv.at[h, :, 0, slot], snd_z.at[h, j], rcv_z.at[h, slot], where)

    def parts_z(h, way):
        return [part_z(h, j, slot, along_z(d, to_zl)) for j, (slot, d, to_zl) in enumerate(way)]

    def part_c(h, d, far):
        sub = slice(3, 4) if far else slice(1, 3)
        src, dst = pkv.at[h, :, 0, sub], pkv.at[h, :, 4 - d, sub]
        return send(src, dst, snd_c.at[far, h, d], rcv_c.at[far, h, d], y_peer[d])

    turn = (2, 1, 3)

    for copy in own_prompt:
        copy.wait()
    for at, way in ((3, upwards), (0, downwards)):

        @pl.when(zl == at)
        def _(way=way):
            for h in range(4):
                for copy in parts_z(h, way):
                    copy.start()

    for d in turn:
        part_own(d).start()

    def to_sib(h):
        far = 1 - k
        return [
            send(q_hbm.at[:, cols(far, h, 512)], qb.at[h, rows], snd_sib.at[h, 0], rcv_sib.at[h, 0], sib),
            send(u_hbm.at[:, cols(far, h, 512)], ub.at[h, rows], snd_sib.at[h, 1], rcv_sib.at[h, 1], sib),
            send(k_hbm.at[:, cols(far, h, 128)], kw.at[h, own_rows], snd_sib.at[h, 2], rcv_sib.at[h, 2], sib),
            send(v_hbm.at[:, cols(far, h, 128)], vw.at[h, own_rows], snd_sib.at[h, 3], rcv_sib.at[h, 3], sib),
        ]

    def halo(h, core, i):
        src, dst = ((k_hbm, kw), (v_hbm, vw))[i]
        return send(
            src.at[:, cols(core, h, 128)], dst.at[h, rows], snd_halo.at[h, core, i], rcv_halo.at[h, k, i], nxt[core]
        )

    for h in range(4):
        for copy in to_sib(h):
            copy.start()

    def halos():
        for h in range(4):
            for core in range(2):
                for i in range(2):
                    halo(h, core, i).start()

    pl.when(x < 3)(halos)

    @pl.when(first)
    def _():
        kw[:, 0:256] = jnp.zeros((4, 256, HD), BF)
        vw[:, 0:256] = jnp.zeros((4, 256, HD), BF)

    @pl.when(last)
    def _():
        gnext[...] = jnp.zeros((8, 2, BLK, HD), BF)

    for copy in small:
        copy.wait()
    base = jnp.maximum(c - 1, 0) * 256
    id_rows = [
        ids[:, pl.ds(pl.multiple_of(base + b * BLK, BLK), BLK)].astype(F32) for b in range(2)
    ] + [ids[:, pl.ds(pl.multiple_of(c * 256 + b * BLK, BLK), BLK)].astype(F32) for b in range(2)]
    wide = [jnp.broadcast_to(r, (BLK, BLK)) for r in id_rows]
    tall = [w.T for w in wide]
    causal1 = causal_block()
    causal = jnp.concatenate([causal1] * 4, 1)
    inside = jnp.where(first, 0, 1)
    for rb in range(2):
        at = 2 * c + rb

        def earlier(step, rb=rb, at=at):
            b = rb + 2 - step
            flag = pat[0, at, jnp.maximum(at - step, 0)]
            if b < 2:
                flag = flag * inside
            return (tall[b] == wide[2 + rb]) & (jnp.full((BLK, BLK), flag, jnp.int32) > 0)

        own = tall[2 + rb] == wide[2 + rb]
        shared = (causal1 & own) | (jnp.logical_not(causal1) & earlier(2))
        for i, seen in enumerate((earlier(1), shared)):
            part = jnp.where(seen, 0.0, HIDE)
            bias[rb, i * BLK : (i + 1) * BLK] = jnp.concatenate([part] * 4, 1)

    def along_y(h, between=None):
        for slot in (1, 2):
            part_z(h, 0, slot, source[slot]).wait_recv()
        for d in turn:
            part_c(h, d, 0).start()
        if between is not None:
            between()
        part_z(h, 0, 3, source[3]).wait_recv()
        for d in turn:
            part_c(h, d, 1).start()

    def late_halos(h):
        pl.when((h == 0) & (x == 3) & jnp.logical_not(last))(halos)

    def window_part(h):
        for copy in own_parts(h):
            copy.wait()
        for copy in to_sib(h):
            copy.wait_recv()

        @pl.when(jnp.logical_not(first))
        def _():
            for core in range(2):
                for i in range(2):
                    dst = (kw, vw)[i].at[h, core * BLK : (core + 1) * BLK]
                    send(dst, dst, snd_halo.at[h, core, i], rcv_halo.at[h, core, i], prv[0]).wait_recv()

        for rb in range(2):
            q = spread(qb[h, rb * BLK : (rb + 1) * BLK])
            u = spread(ub[h, rb * BLK : (rb + 1) * BLK])
            near = slice(rb * BLK, rb * BLK + 384)
            sbuf[h, rb], dbuf[h, rb], top[h, rb] = window_scores(q, u, kw[h, near], vw[h, near], bias[rb], causal)

    early = (x > 0) | first

    @pl.loop(0, 4)
    def _(h):
        pl.when(early)(lambda: window_part(h))

        @pl.when(h < 3)
        def _():
            along_y(h, lambda: late_halos(h))

    for d in turn:
        part_own(d).wait_recv()

    def to_prev(h, core):
        part = gs.at[h, :, core * BLK : (core + 1) * BLK]
        return send(part, gnext.at[k * 4 + h], snd_gprev.at[h, core], rcv_gnext.at[k * 4 + h], prv[core])

    def grads_to_sib(h):
        return send(gs.at[h, :, sib_rows], gown.at[k * 4 + h], snd_gsib.at[h], rcv_gsib.at[h], sib)

    def gq_own(h):
        return pltpu.make_async_copy(gqb.at[h, rows], gq_hbm.at[:, cols(k, h, 512)], sem_gq.at[h])

    def gq_to_sib(h):
        return send(gqb.at[h, other], gq_hbm.at[:, cols(k, h, 512)], snd_gq.at[h], rcv_gq.at[h], sib)

    @pl.loop(0, 4)
    def _(h):
        @pl.when(h == 1)
        def _():
            along_y(3)

        pl.when(jnp.logical_not(early))(lambda: window_part(h))
        for d in turn:
            for far in range(2):
                part_c(h, d, far).wait_recv()

        pk = pkv[h, 0].reshape(512, HD)
        pv = pkv[h, 1].reshape(512, HD)
        pk_t = pk.T
        kw_t = kw[h].T

        a, b = [
            Tile(
                spread(qb[h, rb * BLK : (rb + 1) * BLK]),
                spread(ub[h, rb * BLK : (rb + 1) * BLK]),
                pk, pv, pk_t, kw_t[:, rb * BLK : rb * BLK + 384],
                sbuf.at[h, rb], dbuf.at[h, rb], top[h, rb],
            )
            for rb in range(2)
        ]

        def store_gq(rb, gq):
            for g in range(4):
                gqb[h, rb * BLK : (rb + 1) * BLK, g * HD : (g + 1) * HD] = gq[g * BLK : (g + 1) * BLK]

        for tile in (a, b):
            tile.scores()
        for tile in (a, b):
            tile.expo()
        grads_a, grads_b = a.window(causal), b.window(causal)
        for i in range(2):
            gs[h, i, 0:128] = grads_a[i][0:128].astype(BF)
            gs[h, i, 128:384] = (grads_a[i][128:384] + grads_b[i][0:256]).astype(BF)
            gs[h, i, 384:512] = grads_b[i][256:384].astype(BF)

        @pl.when(jnp.logical_not(first))
        def _():
            to_prev(h, 0).start()
            to_prev(h, 1).start()

        for tile in (a, b):
            tile.dscores()
        for rb, tile in enumerate((a, b)):
            store_gq(rb, tile.grad_queries())

        grads_to_sib(h).start()
        gq_to_sib(h).start()
        gq_own(h).start()
        gown[k * 4 + h] = gs[h, :, own_rows]

    def outs(hh):
        return [
            pltpu.make_async_copy(fin.at[hh, i], out.at[:, hh * HD : (hh + 1) * HD], sem_out.at[hh, i])
            for i, out in enumerate((gk_hbm, gv_hbm))
        ]

    for h in range(4):
        send(gs.at[h, :, sib_rows], gown.at[(1 - k) * 4 + h], snd_gsib.at[h], rcv_gsib.at[h], sib).wait_recv()
        for core in range(2):

            @pl.when(jnp.logical_not(last))
            def _(core=core, h=h):
                part = gnext.at[core * 4 + h]
                send(part, part, snd_gprev.at[h, core], rcv_gnext.at[core * 4 + h], nxt[0]).wait_recv()

            hh = core * 4 + h
            fin[hh] = (gown[hh].astype(F32) + gnext[hh].astype(F32)).astype(BF)
            for copy in outs(hh):
                copy.start()

    for h in range(4):
        gq_own(h).wait()
        copy = gq_to_sib(h)
        copy.wait_send()
        send(gqb.at[h, rows], gq_hbm.at[:, cols(1 - k, h, 512)], snd_gq.at[h], rcv_gq.at[h], sib).wait_recv()
        grads_to_sib(h).wait_send()
        for copy in to_sib(h):
            copy.wait_send()
        for d in (1, 2, 3):
            for far in range(2):
                part_c(h, d, far).wait_send()

    for d in turn:
        part_own(d).wait_send()
    for at, way in ((3, upwards), (0, downwards)):

        @pl.when(zl == at)
        def _(way=way):
            for h in range(4):
                for copy in parts_z(h, way):
                    copy.wait_send()

    @pl.when(jnp.logical_not(last))
    def _():
        for h in range(4):
            for core in range(2):
                for i in range(2):
                    halo(h, core, i).wait_send()

    @pl.when(jnp.logical_not(first))
    def _():
        for h in range(4):
            for core in range(2):
                to_prev(h, core).wait_send()

    for hh in range(KVH):
        for copy in outs(hh):
            copy.wait()


def hand_over(gq, gk, gv, gq_out, gk_out, gv_out, gq_at, gk_at, gv_at, sem_in, sem_out):
    parts = [(ref, slice(0, BLK)) for ref in ((gk, gk_at, gk_out), (gv, gv_at, gv_out))]
    parts += [((gq, gq_at, gq_out), slice(i * 32, (i + 1) * 32)) for i in range(4)]
    loads, stores = [], []
    for i, ((src, at, out), part) in enumerate(parts):
        loads.append(pltpu.make_async_copy(src.at[part], at.at[part], sem_in.at[i]))
        stores.append(pltpu.make_async_copy(at.at[part], out.at[part], sem_out.at[i]))
    for copy in loads:
        copy.start()
    for load, store in zip(loads, stores):
        load.wait()
        store.start()
    for copy in stores:
        copy.wait()


def shards(queries, keys, values, cotangent, prompt_keys, prompt_values, response_ids, block_pattern):
    anywhere = pl.BlockSpec(memory_space=pl.ANY)
    dma = pltpu.SemaphoreType.DMA
    shapes = [jax.ShapeDtypeStruct(a.shape, BF) for a in (queries, keys, values)]
    grads = pl.pallas_call(
        kernel,
        out_shape=shapes,
        in_specs=[anywhere] * 8,
        out_specs=[anywhere] * 3,
        scratch_shapes=[
            pltpu.VMEM((1, 4096), jnp.int32),
            pltpu.SMEM((1, 32, 32), jnp.int32),
            pltpu.VMEM((2, 256, 512), F32),
            pltpu.VMEM((4, 256, 512), BF),
            pltpu.VMEM((4, 256, 512), BF),
            pltpu.VMEM((4, 512, HD), BF),
            pltpu.VMEM((4, 512, HD), BF),
            pltpu.VMEM((4, 2, 4, 4, 32, HD), BF),
            pltpu.VMEM((4, 2, 512, HD), BF),
            pltpu.VMEM((8, 2, BLK, HD), BF),
            pltpu.VMEM((8, 2, BLK, HD), BF),
            pltpu.VMEM((4, 256, 512), BF),
            pltpu.VMEM((8, 2, BLK, HD), BF),
            pltpu.VMEM((4, 2, 256, 512), F32),
            pltpu.VMEM((4, 2, 256, 512), F32),
            pltpu.VMEM((4, 2, 1, 512), F32),
            dma((4, 4)), dma((4,)), dma((1,)),
            dma((4,)), dma((4,)), dma((4, 6)), dma((4, 4)), dma((2, 4, 4)), dma((2, 4, 4)),
            dma((4, 4)), dma((4, 4)), dma((4, 2, 2)), dma((4, 2, 2)), dma((4,)), dma((4,)), dma((4,)),
            dma((4,)), dma((4,)), dma((4, 2)), dma((8,)), dma((8, 2)),
        ],
        compiler_params=pltpu.CompilerParams(
            collective_id=0, has_side_effects=True, vmem_limit_bytes=60 << 20
        ),
        cost_estimate=pl.CostEstimate(flops=4 << 30, bytes_accessed=8 << 20, transcendentals=4 << 20),
        name="tree_attention_backward",
    )(queries, cotangent, keys, values, prompt_keys, prompt_values, response_ids, block_pattern)
    return pl.pallas_call(
        hand_over,
        out_shape=shapes,
        in_specs=[anywhere] * 3,
        out_specs=[anywhere] * 3,
        scratch_shapes=[pltpu.VMEM(a.shape, BF) for a in shapes] + [dma((6,)), dma((6,))],
        compiler_params=pltpu.CompilerParams(vmem_limit_bytes=60 << 20),
        name="hand_over",
    )(*grads)


def solution(mesh):
    tokens = P(("sample", "head"), None)
    prompt = P(None, "sample", None)
    return jax.shard_map(
        shards,
        mesh=mesh,
        in_specs=(tokens, tokens, tokens, tokens, prompt, prompt, P("sample", None), P("sample", None, None)),
        out_specs=(tokens, tokens, tokens),
        check_vma=False,
    )
```

```python
import math

import jax
import jax.numpy as jnp
from jax import lax
from jax.experimental import pallas as pl
from jax.experimental.pallas import tpu as pltpu
from jax.sharding import PartitionSpec as P

KVH = 8
HD = 128
BLK = 128
SCALE = HD**-0.5
SCALE2 = SCALE * math.log2(math.e)
HIDE = -1e30
MESH = pl.DeviceIdType.MESH
BF = jnp.bfloat16
F32 = jnp.float32

NT = (((1,), (1,)), ((), ()))
NN = (((1,), (0,)), ((), ()))


def dot(a, b, dims):
    return lax.dot_general(a, b, dims, preferred_element_type=F32)


def spread(rows):
    return jnp.concatenate([rows[:, g * HD : (g + 1) * HD] for g in range(4)], 0)


def causal_block():
    keys = lax.broadcasted_iota(jnp.int32, (BLK, BLK), 0)
    at = lax.broadcasted_iota(jnp.int32, (BLK, BLK), 1)
    return keys <= at


def window_scores(q, u, kw, vw, bias, causal):
    def products(a, b):
        out = dot(a, b, NT)
        return jnp.concatenate([out[BLK : 2 * BLK], jnp.where(causal, out[2 * BLK :], out[:BLK])], 0)

    sw = products(kw, q) * SCALE2 + bias
    return sw, products(vw, u), jnp.max(sw, 0, keepdims=True)


def unfold(both, causal):
    middle, shared = both[:BLK], both[BLK:]
    zero = jnp.zeros_like(shared)
    return jnp.concatenate([jnp.where(causal, zero, shared), middle, jnp.where(causal, shared, zero)], 0)


class Tile:
    def __init__(self, q, u, pk, pv, pk_t, kw_t, sw, dw, top):
        self.q, self.u, self.pk, self.pv, self.pk_t, self.kw_t = q, u, pk, pv, pk_t, kw_t
        self.sw, self.dw, self.peak = sw, dw, top

    def scores(self):
        self.sp = dot(self.pk, self.q, NT)
        self.peak = jnp.maximum(self.peak, jnp.max(self.sp, 0, keepdims=True) * SCALE2)
        self.dp = dot(self.pv, self.u, NT)

    def expo(self):
        self.ew = jnp.exp2(self.sw[...] - self.peak)
        self.ep = jnp.exp2(self.sp * SCALE2 - self.peak)
        total = jnp.sum(self.ew, 0, keepdims=True) + jnp.sum(self.ep, 0, keepdims=True)
        center = jnp.sum(self.ew * self.dw[...], 0, keepdims=True) + jnp.sum(self.ep * self.dp, 0, keepdims=True)
        self.inv = 1.0 / total
        self.center = center * self.inv

    def window(self, causal):
        w = self.ew * self.inv
        dsw = ((w * SCALE) * (self.dw[...] - self.center)).astype(BF)
        self.dsw = unfold(dsw, causal)
        return dot(self.dsw, self.q, NN), dot(unfold(w.astype(BF), causal), self.u, NN)

    def dscores(self):
        self.ds = (self.ep * (self.dp - self.center)).astype(BF)

    def grad_queries(self):
        prompt = dot(self.pk_t, self.ds, NN) * (self.inv * SCALE)
        return (prompt + dot(self.kw_t, self.dsw, NN)).astype(BF).T


def kernel(
    q_hbm, u_hbm, k_hbm, v_hbm, pk_hbm, pv_hbm, ids_hbm, pat_hbm,
    gq_hbm, gown, gnext,
    ids, pat, bias, qb, ub, kw, vw, pkv, gs, gqb, sbuf, dbuf, top,
    sem_in, sem_small, sem_own,
    snd_own, rcv_own, snd_z, rcv_z, snd_c, rcv_c,
    snd_sib, rcv_sib, snd_halo, rcv_halo, snd_gq, rcv_gq, sem_gq,
    snd_gsib, rcv_gsib, snd_gprev, rcv_gnext, sem_gown,
):
    s = lax.axis_index("sample")
    hd = lax.axis_index("head")
    y, zh = s // 4, s % 4
    c, k = hd // 2, hd % 2
    zl, x = hd // 8, c % 4
    first, last = c == 0, c == 15
    sib = (s, c * 2 + (1 - k))
    nxt = [(s, jnp.minimum(c + 1, 15) * 2 + i) for i in range(2)]
    prv = [(s, jnp.maximum(c - 1, 0) * 2 + i) for i in range(2)]
    column = lax.rem(hd, 8)

    def along_z(d, to_zl):
        return (y * 4 + lax.rem(zh + d, 4), to_zl * 8 + column)

    y_peer = [(lax.rem(y + d, 4) * 4 + zh, hd) for d in range(4)]
    rows = pl.ds(pl.multiple_of(k * BLK, BLK), BLK)
    other = pl.ds(pl.multiple_of((1 - k) * BLK, BLK), BLK)
    own_rows = pl.ds(pl.multiple_of(256 + k * BLK, BLK), BLK)
    sib_rows = pl.ds(pl.multiple_of(256 + (1 - k) * BLK, BLK), BLK)

    def cols(core, h, width):
        return pl.ds(pl.multiple_of((core * 4 + h) * width, BLK), width)

    def send(src, dst, snd, rcv, where):
        return pltpu.make_async_remote_copy(
            src_ref=src, dst_ref=dst, send_sem=snd, recv_sem=rcv, device_id=where, device_id_type=MESH
        )

    barrier = pltpu.get_barrier_semaphore()

    def greet(where):
        pl.semaphore_signal(barrier, inc=1, device_id=where, device_id_type=MESH)

    upwards = [(3, 2, 1), (3, 2, 0), (2, 1, 3), (2, 1, 2), (2, 1, 1), (2, 1, 0)]
    downwards = [(3, 2, 2), (3, 2, 3), (1, 3, 0), (1, 3, 1), (1, 3, 2), (1, 3, 3)]
    source = {1: along_z(1, 0), 2: along_z(3, 3), 3: along_z(2, jnp.where(zl < 2, 3, 0))}
    for where in [sib] + y_peer[1:] + list(source.values()):
        greet(where)

    @pl.when(jnp.logical_not(last))
    def _():
        greet(nxt[0])
        greet(nxt[1])

    @pl.when(jnp.logical_not(first))
    def _():
        greet(prv[0])
        greet(prv[1])

    own_prompt = [
        pltpu.make_async_copy(src.at[pl.ds(k * 4, 4)], pkv.at[:, i, 0, 0], sem_small.at[i])
        for i, src in enumerate((pk_hbm, pv_hbm))
    ]
    for copy in own_prompt:
        copy.start()
    small = [
        pltpu.make_async_copy(ids_hbm, ids, sem_small.at[2]),
        pltpu.make_async_copy(pat_hbm, pat, sem_small.at[3]),
    ]
    for copy in small:
        copy.start()

    def own_parts(h):
        return [
            pltpu.make_async_copy(q_hbm.at[:, cols(k, h, 512)], qb.at[h, rows], sem_in.at[h, 0]),
            pltpu.make_async_copy(u_hbm.at[:, cols(k, h, 512)], ub.at[h, rows], sem_in.at[h, 1]),
            pltpu.make_async_copy(k_hbm.at[:, cols(k, h, 128)], kw.at[h, own_rows], sem_in.at[h, 2]),
            pltpu.make_async_copy(v_hbm.at[:, cols(k, h, 128)], vw.at[h, own_rows], sem_in.at[h, 3]),
        ]

    for h in range(4):
        for copy in own_parts(h):
            copy.start()

    others = 4 + 6 * jnp.where((zl == 0) | (zl == 3), 1, 0) + 2 * jnp.where(first, 0, 1) + 2 * jnp.where(last, 0, 1)
    pl.semaphore_wait(barrier, others)

    def part_own(d):
        return send(pkv.at[:, :, 0, 0], pkv.at[:, :, 4 - d, 0], snd_own.at[d], rcv_own.at[d], y_peer[d])

    def part_z(h, j, slot, where):
        return send(pkv.at[h, :, 0, 0], pkv.at[h, :, 0, slot], snd_z.at[h, j], rcv_z.at[h, slot], where)

    def parts_z(h, way):
        return [part_z(h, j, slot, along_z(d, to_zl)) for j, (slot, d, to_zl) in enumerate(way)]

    def part_c(h, d, far):
        sub = slice(3, 4) if far else slice(1, 3)
        src, dst = pkv.at[h, :, 0, sub], pkv.at[h, :, 4 - d, sub]
        return send(src, dst, snd_c.at[far, h, d], rcv_c.at[far, h, d], y_peer[d])

    turn = (2, 1, 3)

    for copy in own_prompt:
        copy.wait()
    for at, way in ((3, upwards), (0, downwards)):

        @pl.when(zl == at)
        def _(way=way):
            for h in range(4):
                for copy in parts_z(h, way):
                    copy.start()

    for d in turn:
        part_own(d).start()

    def to_sib(h):
        far = 1 - k
        return [
            send(q_hbm.at[:, cols(far, h, 512)], qb.at[h, rows], snd_sib.at[h, 0], rcv_sib.at[h, 0], sib),
            send(u_hbm.at[:, cols(far, h, 512)], ub.at[h, rows], snd_sib.at[h, 1], rcv_sib.at[h, 1], sib),
            send(k_hbm.at[:, cols(far, h, 128)], kw.at[h, own_rows], snd_sib.at[h, 2], rcv_sib.at[h, 2], sib),
            send(v_hbm.at[:, cols(far, h, 128)], vw.at[h, own_rows], snd_sib.at[h, 3], rcv_sib.at[h, 3], sib),
        ]

    def halo(h, core, i):
        src, dst = ((k_hbm, kw), (v_hbm, vw))[i]
        return send(
            src.at[:, cols(core, h, 128)], dst.at[h, rows], snd_halo.at[h, core, i], rcv_halo.at[h, k, i], nxt[core]
        )

    for h in range(4):
        for copy in to_sib(h):
            copy.start()

    def halos():
        for h in range(4):
            for core in range(2):
                for i in range(2):
                    halo(h, core, i).start()

    pl.when(x < 3)(halos)

    @pl.when(first)
    def _():
        kw[:, 0:256] = jnp.zeros((4, 256, HD), BF)
        vw[:, 0:256] = jnp.zeros((4, 256, HD), BF)

    for copy in small:
        copy.wait()
    base = jnp.maximum(c - 1, 0) * 256
    id_rows = [
        ids[:, pl.ds(pl.multiple_of(base + b * BLK, BLK), BLK)].astype(F32) for b in range(2)
    ] + [ids[:, pl.ds(pl.multiple_of(c * 256 + b * BLK, BLK), BLK)].astype(F32) for b in range(2)]
    wide = [jnp.broadcast_to(r, (BLK, BLK)) for r in id_rows]
    tall = [w.T for w in wide]
    causal1 = causal_block()
    causal = jnp.concatenate([causal1] * 4, 1)
    inside = jnp.where(first, 0, 1)
    for rb in range(2):
        at = 2 * c + rb

        def earlier(step, rb=rb, at=at):
            b = rb + 2 - step
            flag = pat[0, at, jnp.maximum(at - step, 0)]
            if b < 2:
                flag = flag * inside
            return (tall[b] == wide[2 + rb]) & (jnp.full((BLK, BLK), flag, jnp.int32) > 0)

        own = tall[2 + rb] == wide[2 + rb]
        shared = (causal1 & own) | (jnp.logical_not(causal1) & earlier(2))
        for i, seen in enumerate((earlier(1), shared)):
            part = jnp.where(seen, 0.0, HIDE)
            bias[rb, i * BLK : (i + 1) * BLK] = jnp.concatenate([part] * 4, 1)

    def along_y(h, between=None):
        for slot in (1, 2):
            part_z(h, 0, slot, source[slot]).wait_recv()
        for d in turn:
            part_c(h, d, 0).start()
        if between is not None:
            between()
        part_z(h, 0, 3, source[3]).wait_recv()
        for d in turn:
            part_c(h, d, 1).start()

    def late_halos(h):
        pl.when((h == 0) & (x == 3) & jnp.logical_not(last))(halos)

    def window_part(h):
        for copy in own_parts(h):
            copy.wait()
        for copy in to_sib(h):
            copy.wait_recv()

        @pl.when(jnp.logical_not(first))
        def _():
            for core in range(2):
                for i in range(2):
                    dst = (kw, vw)[i].at[h, core * BLK : (core + 1) * BLK]
                    send(dst, dst, snd_halo.at[h, core, i], rcv_halo.at[h, core, i], prv[0]).wait_recv()

        for rb in range(2):
            q = spread(qb[h, rb * BLK : (rb + 1) * BLK])
            u = spread(ub[h, rb * BLK : (rb + 1) * BLK])
            near = slice(rb * BLK, rb * BLK + 384)
            sbuf[h, rb], dbuf[h, rb], top[h, rb] = window_scores(q, u, kw[h, near], vw[h, near], bias[rb], causal)

    early = (x > 0) | first

    @pl.loop(0, 4)
    def _(h):
        pl.when(early)(lambda: window_part(h))

        @pl.when(h < 3)
        def _():
            along_y(h, lambda: late_halos(h))

    for d in turn:
        part_own(d).wait_recv()

    def to_prev(h, core):
        part = gs.at[h, :, core * BLK : (core + 1) * BLK]
        return send(part, gnext.at[k * 4 + h], snd_gprev.at[h, core], rcv_gnext.at[k * 4 + h], prv[core])

    def grads_to_sib(h):
        return send(gs.at[h, :, sib_rows], gown.at[k * 4 + h], snd_gsib.at[h], rcv_gsib.at[h], sib)

    def keep(h):
        return pltpu.make_async_copy(gs.at[h, :, own_rows], gown.at[k * 4 + h], sem_gown.at[h])

    def gq_own(h):
        return pltpu.make_async_copy(gqb.at[h, rows], gq_hbm.at[:, cols(k, h, 512)], sem_gq.at[h])

    def gq_to_sib(h):
        return send(gqb.at[h, other], gq_hbm.at[:, cols(k, h, 512)], snd_gq.at[h], rcv_gq.at[h], sib)

    @pl.loop(0, 4)
    def _(h):
        @pl.when(h == 1)
        def _():
            along_y(3)

        pl.when(jnp.logical_not(early))(lambda: window_part(h))
        for d in turn:
            for far in range(2):
                part_c(h, d, far).wait_recv()

        pk = pkv[h, 0].reshape(512, HD)
        pv = pkv[h, 1].reshape(512, HD)
        pk_t = pk.T
        kw_t = kw[h].T

        a, b = [
            Tile(
                spread(qb[h, rb * BLK : (rb + 1) * BLK]),
                spread(ub[h, rb * BLK : (rb + 1) * BLK]),
                pk, pv, pk_t, kw_t[:, rb * BLK : rb * BLK + 384],
                sbuf.at[h, rb], dbuf.at[h, rb], top[h, rb],
            )
            for rb in range(2)
        ]

        def store_gq(rb, gq):
            for g in range(4):
                gqb[h, rb * BLK : (rb + 1) * BLK, g * HD : (g + 1) * HD] = gq[g * BLK : (g + 1) * BLK]

        for tile in (a, b):
            tile.scores()
        for tile in (a, b):
            tile.expo()
        grads_a, grads_b = a.window(causal), b.window(causal)
        for i in range(2):
            gs[h, i, 0:128] = grads_a[i][0:128].astype(BF)
            gs[h, i, 128:384] = (grads_a[i][128:384] + grads_b[i][0:256]).astype(BF)
            gs[h, i, 384:512] = grads_b[i][256:384].astype(BF)

        @pl.when(jnp.logical_not(first))
        def _():
            to_prev(h, 0).start()
            to_prev(h, 1).start()

        for tile in (a, b):
            tile.dscores()
        for rb, tile in enumerate((a, b)):
            store_gq(rb, tile.grad_queries())

        grads_to_sib(h).start()
        gq_to_sib(h).start()
        gq_own(h).start()
        keep(h).start()

    for h in range(4):
        send(gs.at[h, :, sib_rows], gown.at[(1 - k) * 4 + h], snd_gsib.at[h], rcv_gsib.at[h], sib).wait_recv()
        for core in range(2):

            @pl.when(jnp.logical_not(last))
            def _(core=core, h=h):
                part = gnext.at[core * 4 + h]
                send(part, part, snd_gprev.at[h, core], rcv_gnext.at[core * 4 + h], nxt[0]).wait_recv()

    for h in range(4):
        gq_own(h).wait()
        keep(h).wait()
        copy = gq_to_sib(h)
        copy.wait_send()
        send(gqb.at[h, rows], gq_hbm.at[:, cols(1 - k, h, 512)], snd_gq.at[h], rcv_gq.at[h], sib).wait_recv()
        grads_to_sib(h).wait_send()
        for copy in to_sib(h):
            copy.wait_send()
        for d in (1, 2, 3):
            for far in range(2):
                part_c(h, d, far).wait_send()

    for d in turn:
        part_own(d).wait_send()
    for at, way in ((3, upwards), (0, downwards)):

        @pl.when(zl == at)
        def _(way=way):
            for h in range(4):
                for copy in parts_z(h, way):
                    copy.wait_send()

    @pl.when(jnp.logical_not(last))
    def _():
        for h in range(4):
            for core in range(2):
                for i in range(2):
                    halo(h, core, i).wait_send()

    @pl.when(jnp.logical_not(first))
    def _():
        for h in range(4):
            for core in range(2):
                to_prev(h, core).wait_send()


def hand_over(gq, own, nxt, gq_out, gk_out, gv_out, gq_at, gk_at, gv_at, own_at, nxt_at, sem_in, sem_out):
    quarters = [slice(i * 32, (i + 1) * 32) for i in range(4)]
    loads = [pltpu.make_async_copy(own, own_at, sem_in.at[4]), pltpu.make_async_copy(nxt, nxt_at, sem_in.at[5])]
    moves = [pltpu.make_async_copy(gq.at[p], gq_at.at[p], sem_in.at[i]) for i, p in enumerate(quarters)]
    stores = [pltpu.make_async_copy(gq_at.at[p], gq_out.at[p], sem_out.at[i]) for i, p in enumerate(quarters)]
    for copy in loads + moves:
        copy.start()
    for copy in loads:
        copy.wait()
    more = jnp.full((BLK, HD), jnp.where(lax.axis_index("head") // 2 == 15, 0, 1), jnp.int32) > 0
    for i, (at, out) in enumerate(((gk_at, gk_out), (gv_at, gv_out))):
        for hh in range(KVH):
            term = jnp.where(more, nxt_at[hh, i].astype(F32), 0.0)
            at[:, hh * HD : (hh + 1) * HD] = (own_at[hh, i].astype(F32) + term).astype(BF)
        stores.append(pltpu.make_async_copy(at, out, sem_out.at[4 + i]))
        stores[-1].start()
    for load, store in zip(moves, stores):
        load.wait()
        store.start()
    for copy in stores:
        copy.wait()


def shards(queries, keys, values, cotangent, prompt_keys, prompt_values, response_ids, block_pattern):
    anywhere = pl.BlockSpec(memory_space=pl.ANY)
    dma = pltpu.SemaphoreType.DMA
    shapes = [jax.ShapeDtypeStruct(a.shape, BF) for a in (queries, keys, values)]
    window = jax.ShapeDtypeStruct((KVH, 2, BLK, HD), BF)
    grads = pl.pallas_call(
        kernel,
        out_shape=[shapes[0], window, window],
        in_specs=[anywhere] * 8,
        out_specs=[anywhere] * 3,
        scratch_shapes=[
            pltpu.VMEM((1, 4096), jnp.int32),
            pltpu.SMEM((1, 32, 32), jnp.int32),
            pltpu.VMEM((2, 256, 512), F32),
            pltpu.VMEM((4, 256, 512), BF),
            pltpu.VMEM((4, 256, 512), BF),
            pltpu.VMEM((4, 512, HD), BF),
            pltpu.VMEM((4, 512, HD), BF),
            pltpu.VMEM((4, 2, 4, 4, 32, HD), BF),
            pltpu.VMEM((4, 2, 512, HD), BF),
            pltpu.VMEM((4, 256, 512), BF),
            pltpu.VMEM((4, 2, 256, 512), F32),
            pltpu.VMEM((4, 2, 256, 512), F32),
            pltpu.VMEM((4, 2, 1, 512), F32),
            dma((4, 4)), dma((4,)), dma((1,)),
            dma((4,)), dma((4,)), dma((4, 6)), dma((4, 4)), dma((2, 4, 4)), dma((2, 4, 4)),
            dma((4, 4)), dma((4, 4)), dma((4, 2, 2)), dma((4, 2, 2)), dma((4,)), dma((4,)), dma((4,)),
            dma((4,)), dma((4,)), dma((4, 2)), dma((8,)), dma((4,)),
        ],
        compiler_params=pltpu.CompilerParams(
            collective_id=0, has_side_effects=True, vmem_limit_bytes=60 << 20
        ),
        cost_estimate=pl.CostEstimate(flops=4 << 30, bytes_accessed=8 << 20, transcendentals=4 << 20),
        name="tree_attention_backward",
    )(queries, cotangent, keys, values, prompt_keys, prompt_values, response_ids, block_pattern)
    return pl.pallas_call(
        hand_over,
        out_shape=shapes,
        in_specs=[anywhere] * 3,
        out_specs=[anywhere] * 3,
        scratch_shapes=[pltpu.VMEM(a.shape, BF) for a in (*shapes, window, window)] + [dma((6,)), dma((6,))],
        compiler_params=pltpu.CompilerParams(vmem_limit_bytes=60 << 20),
        name="hand_over",
    )(*grads)


def solution(mesh):
    tokens = P(("sample", "head"), None)
    prompt = P(None, "sample", None)
    return jax.shard_map(
        shards,
        mesh=mesh,
        in_specs=(tokens, tokens, tokens, tokens, prompt, prompt, P("sample", None), P("sample", None, None)),
        out_specs=(tokens, tokens, tokens),
        check_vma=False,
    )
```
